32 devices in a mesh: parts: 2 (over x), sec: 8 (over z, y), tile: 2 (over core).
Axes of the slice: x: 2, y: 2, z: 4, core: 2. Of those that a mesh axis runs over, the one named last changes fastest.
Arguments:
- source: bfloat16 [16, 50, 256, 256], P(('parts', 'sec'), 'tile'), parts along dimension 0, may hold values from -6 to 6
- pull_ids: int32 [16, 50, 3], P(('parts', 'sec'), 'tile'), parts along dimension 0, may hold values from 0 to 49, as said below
- interp_idx: int32 [16, 50, 3, 2], P(('parts', 'sec'), 'tile'), parts along dimension 0, may hold values from 0 to 15
- interp_table: bfloat16 [16, 256, 256], replicated, may hold values from -0.375 to 0.375
- patch_pos: int32 [16, 50, 2], P(('parts', 'sec'), 'tile'), parts along dimension 0, may hold values from 0 to 1152
Outputs:
- warped: bfloat16 [16, 2560, 1280], P(('parts', 'sec'), 'tile'), parts along dimension 0
- correlations: float32 [16, 50, 128, 128], P(('parts', 'sec'), 'tile'), parts along dimension 0
The draws below stay inside these ranges and needn't reach their ends.
There are 2 independent parts, one for each index of `parts`. The reference program is written for one: setup_inputs(seed, part) draws one part's arguments, and reference() takes and returns one part's arrays. A program takes and returns all parts, laid end to end along the dimension named above; an argument that names none is the same for every part. Nothing has to cross between parts.
Inputs may be any that keep to these rules, and one draw needn't show every extreme that they name: `pull_ids`: the tile that holds block id b is b // 25. In every tile at least 6 and at most 12 of its 75 pulls name blocks of the other tile of its section, and some tile of every part has exactly 12; the other pulls name its own blocks.
All inputs are finite; a program needn't handle non-finite values.
Results may differ from the reference program's by a relative error of at most 0.012.
Values may be sent and summed in bfloat16 or wider, within the bound.
No kernel may reach another device: no remote copies, remote signals or barrier semaphores. Data moves between devices by JAX's collectives and lax.ppermute only.
A program may use at most 128 MiB of HBM per device.

```python
import jax
import jax.numpy as jnp
from jax import lax

BS = 256
PS = 128
GRID = 5
KP = 3
NMAT = 16
BLOCKS_DEV = 25
PATCHES_DEV = 25
TILE_PIX = 1280
CAP = 12
SECTIONS = 8
TILES = 2
SEC_BLOCKS = 50


def draw_pull_ids(key, part):
    key = jax.random.fold_in(key, 7)
    key_count, key_full, key_order, key_local = jax.random.split(key, 4)
    pull_count = BLOCKS_DEV * KP
    counts = jax.random.randint(key_count, (SECTIONS, TILES), CAP // 2, CAP + 1)
    chosen = jax.random.randint(key_full, (), 0, SECTIONS * TILES)
    flat_index = jnp.arange(SECTIONS * TILES).reshape(SECTIONS, TILES)
    counts = jnp.where(flat_index == chosen, CAP, counts)
    order_keys = jax.random.split(key_order, SECTIONS * TILES)
    orders = jax.vmap(lambda single: jax.random.permutation(single, pull_count))(order_keys)
    orders = orders.reshape(SECTIONS, TILES, pull_count)
    remote = orders < counts[:, :, None]
    home = jnp.arange(TILES).reshape(1, TILES, 1)
    owning = jnp.where(remote, (home + 1) % TILES, home)
    local_index = jax.random.randint(key_local, (SECTIONS, TILES, pull_count), 0, BLOCKS_DEV)
    block_ids = owning * BLOCKS_DEV + local_index
    return block_ids.reshape(SECTIONS, TILES * BLOCKS_DEV, KP).astype(jnp.int32)


def with_ends(drawn, stream_key, least, high):
    shape = drawn.shape
    index_at = [jax.random.randint(jax.random.fold_in(stream_key, axis), (), 0, shape[axis]) for axis in range(len(shape))]
    drawn = drawn.at[tuple(index_at)].set(least)
    longest = shape.index(max(shape))
    index_at[longest] = (index_at[longest] + 1) % shape[longest]
    return drawn.at[tuple(index_at)].set(high)


def block_scale(rng, extent, cuts, least, largest):
    def one(position, blocks):
        steps = jax.random.uniform(jax.random.fold_in(jax.random.fold_in(rng, 6), position), (blocks,), jnp.float32, least / len(cuts), largest / len(cuts))
        return jnp.repeat(jnp.exp(steps), extent[position] // blocks).reshape((-1,) + (1,) * (len(extent) - position - 1))

    level = one(*cuts[0])
    for cut in cuts[1:]:
        level = level * one(*cut)
    return level


def normal_values(stream_key, shape, spread, bound, shards=(), dtype=jnp.bfloat16):
    result = spread * jax.random.normal(stream_key, shape, jnp.float32)
    if shards:
        result = result * block_scale(stream_key, shape, shards, -0.22, 0.18)
    return jnp.clip(result, -bound, bound).astype(dtype)


def setup_inputs(seed: int = 0, part: int = 0) -> dict:
    splits = jax.random.split(jax.random.key(seed), 6)
    own_keys = jax.random.split(jax.random.fold_in(splits[5], part), 6)
    return {
        "source": normal_values(own_keys[0], (SECTIONS, SEC_BLOCKS, BS, BS), 1.0, 6.0, ((0, 8), (1, 2))),
        "pull_ids": draw_pull_ids(jax.random.fold_in(jax.random.fold_in(splits[5], part), 71), part),
        "interp_idx": with_ends(jax.random.randint(own_keys[2], (SECTIONS, TILES * BLOCKS_DEV, KP, 2), 0, NMAT), jax.random.fold_in(own_keys[2], 1), 0, NMAT - 1).astype(jnp.int32),
        "interp_table": normal_values(splits[3], (NMAT, BS, BS), BS ** -0.5, 0.375),
        "patch_pos": with_ends(jax.random.randint(own_keys[4], (SECTIONS, TILES * PATCHES_DEV, 2), 0, TILE_PIX - PS + 1), jax.random.fold_in(own_keys[4], 1), 0, TILE_PIX - PS).astype(jnp.int32),
    }


EPSILON = 1e-06

def warp_tile(section_blocks, block_ids, matrix_index, interp_table):
    pulled = section_blocks[block_ids]
    row_mats = interp_table[matrix_index[:, 0]].astype(jnp.float32)
    col_mats = interp_table[matrix_index[:, 1]].astype(jnp.float32)
    left_product = jnp.einsum('rij,rjk->rik', row_mats, pulled.astype(jnp.float32)).astype(jnp.bfloat16)
    summed_terms = jnp.einsum('rik,rlk->ril', left_product.astype(jnp.float32), col_mats)
    blocks_out = summed_terms.reshape(BLOCKS_DEV, KP, BS, BS).sum(axis=1).astype(jnp.bfloat16)
    return blocks_out.reshape(GRID, GRID, BS, BS).transpose(0, 2, 1, 3).reshape(TILE_PIX, TILE_PIX)

def extract(picture, corners):
    return jax.vmap(lambda corner: lax.dynamic_slice(picture, (corner[0], corner[1]), (PS, PS)))(corners)

def correlate(own_patches, previous):
    first = own_patches.astype(jnp.float32)
    first = first - lax.optimization_barrier(jnp.mean(first, axis=(1, 2), keepdims=True))
    second = previous.astype(jnp.float32)
    second = second - lax.optimization_barrier(jnp.mean(second, axis=(1, 2), keepdims=True))
    cross = jnp.fft.fft2(first) * jnp.conj(jnp.fft.fft2(second))
    circular = jnp.real(jnp.fft.ifft2(cross))
    scale = PS * jnp.sqrt((lax.optimization_barrier(jnp.mean(first * first, axis=(1, 2))) + EPSILON) * (lax.optimization_barrier(jnp.mean(second * second, axis=(1, 2))) + EPSILON))
    return circular / scale[:, None, None]

def reference(source, pull_ids, interp_idx, interp_table, patch_pos):
    id_rows = pull_ids.reshape(SECTIONS, TILES, BLOCKS_DEV * KP)
    matrix_rows = interp_idx.reshape(SECTIONS, TILES, BLOCKS_DEV * KP, 2)

    def one_section(packed):
        section_blocks, section_ids, section_mats = packed
        return lax.map(lambda pair: warp_tile(section_blocks, pair[0], pair[1], interp_table), (section_ids, section_mats))
    tiles_out = lax.map(one_section, (source, id_rows, matrix_rows))
    earlier = jnp.concatenate([jnp.zeros_like(tiles_out[:1]), tiles_out[:-1]], axis=0)
    corner_rows = patch_pos.reshape(SECTIONS, TILES, PATCHES_DEV, 2)

    def match_section(packed):
        current, before, corners = packed

        def match_tile(inner):
            return correlate(extract(inner[0], inner[2]), extract(inner[1], inner[2]))
        return lax.map(match_tile, (current, before, corners))
    scores = lax.map(match_section, (tiles_out, earlier, corner_rows))
    warped = tiles_out.reshape(SECTIONS, TILES * TILE_PIX, TILE_PIX)
    correlations = scores.reshape(SECTIONS, TILES * PATCHES_DEV, PS, PS)
    return (warped, correlations)
```

```python
import functools

import jax
import jax.numpy as jnp
import ml_dtypes
import numpy as np
from jax import lax
from jax.experimental import pallas as pl
from jax.experimental.pallas import tpu as pltpu
from jax.sharding import PartitionSpec as P

BS = 256
PS = 128
KP = 3
EPSILON = 1e-06
CAP = 12
ROWS = PS + 16
COLS = 2 * PS

SMEM = pl.BlockSpec(memory_space=pltpu.SMEM)
VMEM = pl.BlockSpec(memory_space=pltpu.VMEM)
ANY = pl.BlockSpec(memory_space=pl.ANY)
F32 = jnp.float32
BF16 = jnp.bfloat16


def tables():
    grid = np.arange(PS)
    angle = 2.0 * np.pi / PS * (grid[:, None] * grid[None, :] % PS)
    cosine, sine = np.cos(angle), np.sin(angle)
    across = np.concatenate([cosine, sine], axis=1)
    high = across.astype(ml_dtypes.bfloat16)
    low = (across - high.astype(np.float64)).astype(ml_dtypes.bfloat16)
    forward = np.concatenate([high, low], axis=0)
    constant = forward.astype(np.float64).sum(axis=0, keepdims=True).astype(np.float32)
    down = np.block([[cosine, -sine], [sine, cosine]]).astype(ml_dtypes.bfloat16)
    back = np.concatenate([cosine, -sine], axis=0).astype(ml_dtypes.bfloat16)
    return forward, constant, down, back


def dot(a, b):
    return jnp.dot(a, b, preferred_element_type=F32)


def block_order(ids, order, tile, count):
    first, last = jnp.int32(0), jnp.int32(count - 1)
    for b in range(count):
        away = (ids[b, 0] // count != tile) | (ids[b, 1] // count != tile) | (ids[b, 2] // count != tile)
        order[jnp.where(away, last, first)] = b
        first = first + jnp.where(away, 0, 1)
        last = last - jnp.where(away, 1, 0)


def place(block, grid):
    row = pl.multiple_of(block // grid * BS, BS)
    col = pl.multiple_of(block % grid * BS, BS)
    return pl.ds(row, BS), pl.ds(col, BS)


def warp_blocks(blocks, ids, mats, table, slots, arrived, finish):
    for n, block in enumerate(blocks):
        for k in range(KP):
            arrived(n, k)
        total = None
        for k in range(KP):
            left = dot(table[mats[block, 2 * k]], slots[n * KP + k]).astype(BF16)
            term = lax.dot_general(
                left, table[mats[block, 2 * k + 1]], (((1,), (1,)), ((), ())), preferred_element_type=F32
            )
            total = term if total is None else total + term
        finish(n, block, total.astype(BF16))


def near_kernel(count, grid, ids, mats, source, table, warped, order, slots, done, in_sem, out_sem):
    tile = lax.axis_index("tile")
    near = count - CAP
    block_order(ids, order, tile, count)
    blocks = [order[n] for n in range(near)]

    def fetch(n, k):
        index = ids[blocks[n], k] - tile * count
        return pltpu.make_async_copy(source.at[index], slots.at[n * KP + k], in_sem.at[n * KP + k])

    for n in range(near):
        for k in range(KP):
            fetch(n, k).start()
    writes = []

    def finish(n, block, value):
        done[n] = value
        writes.append(pltpu.make_async_copy(done.at[n], warped.at[place(block, grid)], out_sem.at[n]))
        writes[-1].start()

    warp_blocks(blocks, ids, mats, table, slots, lambda n, k: fetch(n, k).wait(), finish)
    for write in writes:
        write.wait()


def window(picture, y, x):
    top = pl.multiple_of(jnp.minimum(y // 16 * 16, picture.shape[0] - ROWS), 16)
    left = pl.multiple_of(jnp.minimum(x // PS * PS, picture.shape[1] - COLS), PS)
    area = picture[pl.ds(top, ROWS), pl.ds(left, COLS)]
    i = lax.broadcasted_iota(jnp.int32, (PS, ROWS), 0)
    r = lax.broadcasted_iota(jnp.int32, (PS, ROWS), 1)
    pick_rows = (r - i == y - top).astype(F32).astype(BF16)
    c = lax.broadcasted_iota(jnp.int32, (COLS, PS), 0)
    j = lax.broadcasted_iota(jnp.int32, (COLS, PS), 1)
    pick_cols = (c - j == x - left).astype(F32).astype(BF16)
    return dot(dot(pick_rows, area).astype(BF16), pick_cols).astype(BF16)


def far_kernel(
    count, grid, patches, ids, mats, corners, source, other, table, begun, warped, out,
    order, slots, picture, in_sem, near_sem, out_sem,
):
    tile = lax.axis_index("tile")
    near = count - CAP
    block_order(ids, order, tile, count)
    blocks = [order[near + n] for n in range(CAP)]

    def fetch(n, k, act):
        index = ids[blocks[n], k]
        home = index // count
        slot, sem = slots.at[n * KP + k], in_sem.at[n * KP + k]

        @pl.when(home == tile)
        def _():
            act(pltpu.make_async_copy(source.at[index - home * count], slot, sem))

        @pl.when(home != tile)
        def _():
            act(pltpu.make_async_copy(other.at[index - home * count], slot, sem))

    for n in range(CAP):
        for k in range(KP):
            fetch(n, k, lambda copy: copy.start())
    loads = []
    for n in range(near):
        at = place(order[n], grid)
        loads.append(pltpu.make_async_copy(begun.at[at], picture.at[at], near_sem.at[n]))
        loads[-1].start()
    writes = []

    def arrived(n, k):
        pltpu.make_async_copy(source.at[0], slots.at[n * KP + k], in_sem.at[n * KP + k]).wait()

    def finish(n, block, value):
        at = place(block, grid)
        picture[at] = value
        writes.append(pltpu.make_async_copy(picture.at[at], warped.at[at], out_sem.at[n]))
        writes[-1].start()

    warp_blocks(blocks, ids, mats, table, slots, arrived, finish)
    for load in loads:
        load.wait()
    for p in range(patches):
        out[p] = window(picture, corners[p, 0], corners[p, 1])
    for write in writes:
        write.wait()


def spectrum_columns(patch, forward, constant):
    values = patch.astype(F32)
    mean = jnp.sum(values, keepdims=True) * (1.0 / (PS * PS))
    centred = values - mean
    power = jnp.sum(centred * centred, keepdims=True) * (1.0 / (PS * PS))
    halves = dot(jnp.concatenate([patch, patch], axis=1), forward[...]) - mean * constant[...]
    halves = halves.astype(BF16)
    return halves[:, :PS], halves[:, PS:], power


def own_kernel(patches, corners, picture, forward, constant, down, out, power_out):
    for p in range(patches):
        patch = window(picture, corners[p, 0], corners[p, 1])
        cosine_part, sine_part, power = spectrum_columns(patch, forward, constant)
        out[p] = dot(down[...], jnp.concatenate([cosine_part, sine_part], axis=0))
        power_out[pl.ds(p, 1), :] = jnp.broadcast_to(power, (1, PS))


def match_kernel(patches, previous, spectra, powers, forward, constant, down, back, out):
    for start in range(0, patches, 2):
        pair = range(start, min(start + 2, patches))
        parts = [spectrum_columns(previous[p], forward, constant) for p in pair]
        stacked = jnp.concatenate(
            [jnp.concatenate([part[h] for part in parts], axis=1) for h in range(2)], axis=0
        )
        second = dot(down[...], stacked)
        crosses = []
        for n, p in enumerate(pair):
            one_real, one_imag = spectra[p, :PS, :], spectra[p, PS:, :]
            two_real, two_imag = second[:PS, n * PS : (n + 1) * PS], second[PS:, n * PS : (n + 1) * PS]
            real = one_real * two_real + one_imag * two_imag
            imag = one_real * two_imag - one_imag * two_real
            crosses.append(jnp.concatenate([real.astype(BF16), imag.astype(BF16)], axis=0))
        mixed = dot(down[...], jnp.concatenate(crosses, axis=1)).astype(BF16)
        for n, p in enumerate(pair):
            real, imag = mixed[:PS, n * PS : (n + 1) * PS], mixed[PS:, n * PS : (n + 1) * PS]
            circular = dot(jnp.concatenate([real, imag], axis=1), back[...])
            product = (powers[pl.ds(p, 1), :] + EPSILON) * (parts[n][2] + EPSILON)
            out[p] = circular * (lax.rsqrt(product) * (1.0 / (PS * PS * PS)))


def params(megabytes, flops, moved):
    return dict(
        compiler_params=pltpu.CompilerParams(vmem_limit_bytes=megabytes << 20),
        cost_estimate=pl.CostEstimate(flops=flops, bytes_accessed=moved, transcendentals=0),
    )


def shards(source, pull_ids, interp_idx, interp_table, patch_pos):
    blocks = source[0]
    count = blocks.shape[0]
    grid = int(round(count**0.5))
    patches = patch_pos.shape[1]
    side = grid * BS
    near = count - CAP
    ids = pull_ids[0]
    mats = interp_idx[0].reshape(count, 2 * KP)
    positions = patch_pos[0]
    sections = lax.axis_size("sec")
    tiles = lax.axis_size("tile")
    other = lax.ppermute(blocks, "tile", [(i, (i + 1) % tiles) for i in range(tiles)])
    wanted = lax.ppermute(positions, "sec", [(i + 1, i) for i in range(sections - 1)])
    forward, constant, down, back = tables()

    begun = pl.pallas_call(
        functools.partial(near_kernel, count, grid),
        out_shape=jax.ShapeDtypeStruct((side, side), BF16),
        in_specs=[SMEM, SMEM, ANY, VMEM],
        out_specs=ANY,
        scratch_shapes=[
            pltpu.SMEM((count,), jnp.int32),
            pltpu.VMEM((near * KP, BS, BS), BF16),
            pltpu.VMEM((near, BS, BS), BF16),
            pltpu.SemaphoreType.DMA((near * KP,)),
            pltpu.SemaphoreType.DMA((near,)),
        ],
        **params(20, near * KP * 4 * BS**3, near * (KP + 1) * BS * BS * 2),
    )(ids, mats, blocks, interp_table)

    warped, sent = pl.pallas_call(
        functools.partial(far_kernel, count, grid, patches),
        out_shape=(
            jax.ShapeDtypeStruct((side, side), BF16),
            jax.ShapeDtypeStruct((patches, PS, PS), BF16),
        ),
        in_specs=[SMEM, SMEM, SMEM, ANY, ANY, VMEM, ANY],
        out_specs=(ANY, VMEM),
        scratch_shapes=[
            pltpu.SMEM((count,), jnp.int32),
            pltpu.VMEM((CAP * KP, BS, BS), BF16),
            pltpu.VMEM((side, side), BF16),
            pltpu.SemaphoreType.DMA((CAP * KP,)),
            pltpu.SemaphoreType.DMA((near,)),
            pltpu.SemaphoreType.DMA((CAP,)),
        ],
        input_output_aliases={6: 0},
        **params(24, CAP * KP * 4 * BS**3, CAP * (KP + 1) * BS * BS * 2),
    )(ids, mats, wanted, blocks, other, interp_table, begun)

    previous = lax.ppermute(sent, "sec", [(i, i + 1) for i in range(sections - 1)])

    spectra, powers = pl.pallas_call(
        functools.partial(own_kernel, patches),
        out_shape=(
            jax.ShapeDtypeStruct((patches, 2 * PS, PS), F32),
            jax.ShapeDtypeStruct((patches, PS), F32),
        ),
        in_specs=[SMEM] + [VMEM] * 4,
        out_specs=(VMEM, VMEM),
        **params(20, patches * 12 * PS**3, side * side * 2),
    )(positions, warped, forward, constant, down)

    correlations = pl.pallas_call(
        functools.partial(match_kernel, patches),
        out_shape=jax.ShapeDtypeStruct((patches, PS, PS), F32),
        in_specs=[VMEM] * 7,
        out_specs=VMEM,
        **params(20, patches * 16 * PS**3, patches * PS * PS * 14),
    )(previous, spectra, powers, forward, constant, down, back)
    return warped[None], correlations[None]


def solution(mesh):
    return jax.shard_map(
        shards,
        mesh=mesh,
        in_specs=(
            P(("parts", "sec"), "tile", None, None),
            P(("parts", "sec"), "tile", None),
            P(("parts", "sec"), "tile", None, None),
            P(),
            P(("parts", "sec"), "tile", None),
        ),
        out_specs=(P(("parts", "sec"), "tile", None), P(("parts", "sec"), "tile", None, None)),
        check_vma=False,
    )
```

```python
import functools

import jax
import jax.numpy as jnp
import ml_dtypes
import numpy as np
from jax import lax
from jax.experimental import pallas as pl
from jax.experimental.pallas import tpu as pltpu
from jax.sharding import PartitionSpec as P

BS = 256
PS = 128
KP = 3
EPSILON = 1e-06
CAP = 12
ROWS = PS + 16
COLS = 2 * PS

SMEM = pl.BlockSpec(memory_space=pltpu.SMEM)
VMEM = pl.BlockSpec(memory_space=pltpu.VMEM)
ANY = pl.BlockSpec(memory_space=pl.ANY)
F32 = jnp.float32
BF16 = jnp.bfloat16


def tables():
    grid = np.arange(PS)
    angle = 2.0 * np.pi / PS * (grid[:, None] * grid[None, :] % PS)
    cosine, sine = np.cos(angle), np.sin(angle)
    across = np.concatenate([cosine, sine], axis=1)
    high = across.astype(ml_dtypes.bfloat16)
    low = (across - high.astype(np.float64)).astype(ml_dtypes.bfloat16)
    forward = np.concatenate([high, low], axis=0)
    constant = forward.astype(np.float64).sum(axis=0, keepdims=True).astype(np.float32)
    down = np.block([[cosine, -sine], [sine, cosine]]).astype(ml_dtypes.bfloat16)
    back = np.concatenate([cosine, -sine], axis=0).astype(ml_dtypes.bfloat16)
    return forward, constant, down, back


def dot(a, b):
    return jnp.dot(a, b, preferred_element_type=F32)


def block_order(ids, order, low, count):
    first, last = jnp.int32(0), jnp.int32(count - 1)
    for b in range(count):
        near = None
        for k in range(KP):
            local = ids[k, b] - low
            here = (local >= 0) & (local < count)
            near = here if near is None else near & here
        order[jnp.where(near, first, last)] = b
        step = near.astype(jnp.int32)
        first = first + step
        last = last + step - 1


def place(block, grid):
    row = pl.multiple_of(block // grid * BS, BS)
    col = pl.multiple_of(block % grid * BS, BS)
    return pl.ds(row, BS), pl.ds(col, BS)


def warp_block(block, mats, table, pulled):
    total = None
    for k in range(KP):
        left = dot(table[mats[k, 0, block]], pulled(k)).astype(BF16)
        term = lax.dot_general(
            left, table[mats[k, 1, block]], (((1,), (1,)), ((), ())), preferred_element_type=F32
        )
        total = term if total is None else total + term
    return total.astype(BF16)


def near_kernel(count, ids, mats, source, table, begun, order):
    low = lax.axis_index("tile") * count
    block_order(ids, order, low, count)
    for n in range(count - CAP):
        block = order[n]
        begun[n] = warp_block(block, mats, table, lambda k: source[ids[k, block] - low])


def window(picture, y, x):
    top = pl.multiple_of(jnp.minimum(y // 16 * 16, picture.shape[0] - ROWS), 16)
    left = pl.multiple_of(jnp.minimum(x // PS * PS, picture.shape[1] - COLS), PS)
    area = picture[pl.ds(top, ROWS), pl.ds(left, COLS)]
    i = lax.broadcasted_iota(jnp.int32, (PS, ROWS), 0)
    r = lax.broadcasted_iota(jnp.int32, (PS, ROWS), 1)
    pick_rows = (r - i == y - top).astype(F32).astype(BF16)
    c = lax.broadcasted_iota(jnp.int32, (COLS, PS), 0)
    j = lax.broadcasted_iota(jnp.int32, (COLS, PS), 1)
    pick_cols = (c - j == x - left).astype(F32).astype(BF16)
    return dot(dot(pick_rows, area).astype(BF16), pick_cols).astype(BF16)


def far_kernel(
    count, grid, patches, ids, mats, corners, source, other, table, begun, picture, out, order
):
    tile = lax.axis_index("tile")
    low = tile * count
    there = (1 - tile) * count
    near = count - CAP
    block_order(ids, order, low, count)
    for n in range(near):
        picture[place(order[n], grid)] = begun[n]
    for n in range(near, count):
        block = order[n]

        def pulled(k):
            index = ids[k, block]
            local = index - low
            here = (local >= 0) & (local < count)
            own = source[jnp.where(here, local, 0)]
            return jnp.where(here, own, other[jnp.where(here, 0, index - there)])

        picture[place(block, grid)] = warp_block(block, mats, table, pulled)
    for p in range(patches):
        out[p] = window(picture, corners[0, p], corners[1, p])


def spectrum_columns(patch, forward, constant):
    values = patch.astype(F32)
    mean = jnp.sum(values, keepdims=True) * (1.0 / (PS * PS))
    centred = values - mean
    power = jnp.sum(centred * centred, keepdims=True) * (1.0 / (PS * PS))
    halves = dot(jnp.concatenate([patch, patch], axis=1), forward[...]) - mean * constant[...]
    halves = halves.astype(BF16)
    return halves[:, :PS], halves[:, PS:], power


def own_kernel(patches, corners, picture, forward, constant, down, out, power_out):
    for p in range(patches):
        patch = window(picture, corners[0, p], corners[1, p])
        cosine_part, sine_part, power = spectrum_columns(patch, forward, constant)
        out[p] = dot(down[...], jnp.concatenate([cosine_part, sine_part], axis=0))
        power_out[pl.ds(p, 1), :] = jnp.broadcast_to(power, (1, PS))


def match_kernel(patches, previous, spectra, powers, forward, constant, down, back, out, halves, crosses, mixed, scales):
    for p in range(patches):
        cosine_part, sine_part, power = spectrum_columns(previous[p], forward, constant)
        at = pl.ds(p % 2 * PS, PS)
        halves[p // 2, :PS, at] = cosine_part
        halves[p // 2, PS:, at] = sine_part
        product = (powers[pl.ds(p, 1), :] + EPSILON) * (power + EPSILON)
        scales[pl.ds(p, 1), :] = lax.rsqrt(product) * (1.0 / (PS * PS * PS))
    pairs = [range(start, min(start + 2, patches)) for start in range(0, patches, 2)]
    for q, pair in enumerate(pairs):
        width = PS * len(pair)
        second = dot(down[...], halves[q, :, :width])
        for n, p in enumerate(pair):
            one_real, one_imag = spectra[p, :PS, :], spectra[p, PS:, :]
            two_real, two_imag = second[:PS, n * PS : (n + 1) * PS], second[PS:, n * PS : (n + 1) * PS]
            real = one_real * two_real + one_imag * two_imag
            imag = one_real * two_imag - one_imag * two_real
            crosses[q, :PS, pl.ds(n * PS, PS)] = real.astype(BF16)
            crosses[q, PS:, pl.ds(n * PS, PS)] = imag.astype(BF16)
    for q, pair in enumerate(pairs):
        width = PS * len(pair)
        both = dot(down[...], crosses[q, :, :width]).astype(BF16)
        for n, p in enumerate(pair):
            mixed[p, :, :PS] = both[:PS, n * PS : (n + 1) * PS]
            mixed[p, :, PS:] = both[PS:, n * PS : (n + 1) * PS]
    for p in range(patches):
        out[p] = dot(mixed[p], back[...]) * scales[pl.ds(p, 1), :]


def params(megabytes, flops, moved):
    return dict(
        compiler_params=pltpu.CompilerParams(vmem_limit_bytes=megabytes << 20),
        cost_estimate=pl.CostEstimate(flops=flops, bytes_accessed=moved, transcendentals=0),
    )


def shards(source, pull_ids, interp_idx, interp_table, patch_pos):
    blocks = source[0]
    count = blocks.shape[0]
    grid = int(round(count**0.5))
    patches = patch_pos.shape[1]
    side = grid * BS
    near = count - CAP
    ids = pull_ids[0].T
    mats = interp_idx[0].transpose(1, 2, 0)
    positions = patch_pos[0].T
    sections = lax.axis_size("sec")
    tiles = lax.axis_size("tile")
    other = lax.ppermute(blocks, "tile", [(i, (i + 1) % tiles) for i in range(tiles)])
    wanted = lax.ppermute(positions, "sec", [(i + 1, i) for i in range(sections - 1)])
    forward, constant, down, back = tables()

    begun = pl.pallas_call(
        functools.partial(near_kernel, count),
        out_shape=jax.ShapeDtypeStruct((near, BS, BS), BF16),
        in_specs=[SMEM, SMEM, VMEM, VMEM],
        out_specs=VMEM,
        scratch_shapes=[pltpu.SMEM((count,), jnp.int32)],
        **params(16, near * KP * 4 * BS**3, near * (KP + 1) * BS * BS * 2),
    )(ids, mats, blocks, interp_table)

    warped, sent = pl.pallas_call(
        functools.partial(far_kernel, count, grid, patches),
        out_shape=(
            jax.ShapeDtypeStruct((side, side), BF16),
            jax.ShapeDtypeStruct((patches, PS, PS), BF16),
        ),
        in_specs=[SMEM] * 3 + [VMEM] * 4,
        out_specs=(VMEM, VMEM),
        scratch_shapes=[pltpu.SMEM((count,), jnp.int32)],
        **params(16, CAP * KP * 4 * BS**3, CAP * (KP + 1) * BS * BS * 2),
    )(ids, mats, wanted, blocks, other, interp_table, begun)

    previous = lax.ppermute(sent, "sec", [(i, i + 1) for i in range(sections - 1)])

    spectra, powers = pl.pallas_call(
        functools.partial(own_kernel, patches),
        out_shape=(
            jax.ShapeDtypeStruct((patches, 2 * PS, PS), F32),
            jax.ShapeDtypeStruct((patches, PS), F32),
        ),
        in_specs=[SMEM] + [VMEM] * 4,
        out_specs=(VMEM, VMEM),
        **params(20, patches * 12 * PS**3, side * side * 2),
    )(positions, warped, forward, constant, down)

    correlations = pl.pallas_call(
        functools.partial(match_kernel, patches),
        out_shape=jax.ShapeDtypeStruct((patches, PS, PS), F32),
        in_specs=[VMEM] * 7,
        out_specs=VMEM,
        scratch_shapes=[
            pltpu.VMEM(((patches + 1) // 2, 2 * PS, 2 * PS), BF16),
            pltpu.VMEM(((patches + 1) // 2, 2 * PS, 2 * PS), BF16),
            pltpu.VMEM((patches, PS, 2 * PS), BF16),
            pltpu.VMEM((patches, PS), F32),
        ],
        **params(20, patches * 16 * PS**3, patches * PS * PS * 14),
    )(previous, spectra, powers, forward, constant, down, back)
    return warped[None], correlations[None]


def solution(mesh):
    return jax.shard_map(
        shards,
        mesh=mesh,
        in_specs=(
            P(("parts", "sec"), "tile", None, None),
            P(("parts", "sec"), "tile", None),
            P(("parts", "sec"), "tile", None, None),
            P(),
            P(("parts", "sec"), "tile", None),
        ),
        out_specs=(P(("parts", "sec"), "tile", None), P(("parts", "sec"), "tile", None, None)),
        check_vma=False,
    )
```

```python
import functools

import jax
import jax.numpy as jnp
import ml_dtypes
import numpy as np
from jax import lax
from jax.experimental import pallas as pl
from jax.experimental.pallas import tpu as pltpu
from jax.sharding import PartitionSpec as P

BS = 256
PS = 128
KP = 3
EPSILON = 1e-06
CAP = 12
ROWS = PS + 16
COLS = 2 * PS
PARTS = (0.64,)

SMEM = pl.BlockSpec(memory_space=pltpu.SMEM)
VMEM = pl.BlockSpec(memory_space=pltpu.VMEM)
ANY = pl.BlockSpec(memory_space=pl.ANY)
F32 = jnp.float32
BF16 = jnp.bfloat16


def tables():
    grid = np.arange(PS)
    angle = 2.0 * np.pi / PS * (grid[:, None] * grid[None, :] % PS)
    cosine, sine = np.cos(angle), np.sin(angle)
    across = np.concatenate([cosine, sine], axis=1)
    high = across.astype(ml_dtypes.bfloat16)
    low = (across - high.astype(np.float64)).astype(ml_dtypes.bfloat16)
    forward = np.concatenate([high, low], axis=0)
    constant = forward.astype(np.float64).sum(axis=0, keepdims=True).astype(np.float32)
    down = np.block([[cosine, -sine], [sine, cosine]]).astype(ml_dtypes.bfloat16)
    back = np.concatenate([cosine, -sine], axis=0).astype(ml_dtypes.bfloat16)
    return forward, constant, down, back


def dot(a, b):
    return jnp.dot(a, b, preferred_element_type=F32)


FIELDS = 1 + 3 * KP


def plan_kernel(count, tiles, ids_from, mats_from, plan, ids, mats, sems):
    copies = [
        pltpu.make_async_copy(ids_from, ids, sems.at[0]),
        pltpu.make_async_copy(mats_from, mats, sems.at[1]),
    ]
    for copy in copies:
        copy.start()
    for copy in copies:
        copy.wait()
    low = lax.axis_index("tile") * count
    first, last = jnp.int32(0), jnp.int32(count - 1)
    for b in range(count):
        near, pulls = None, []
        for k in range(KP):
            local = ids[k, 0, b] - low
            here = (local >= 0) & (local < count)
            near = here if near is None else near & here
            pulls.append(jnp.where(local < 0, local + tiles * count, local))
        step = near.astype(jnp.int32)
        at = (last + step * (first - last)) * FIELDS
        first = first + step
        last = last + step - 1
        plan[at] = b
        for k in range(KP):
            plan[at + 1 + 3 * k] = pulls[k]
            plan[at + 2 + 3 * k] = mats[k, 0, b]
            plan[at + 3 + 3 * k] = mats[k, 1, b]


def place(block, grid):
    row = pl.multiple_of(block // grid * BS, BS)
    col = pl.multiple_of(block % grid * BS, BS)
    return pl.ds(row, BS), pl.ds(col, BS)


def warp_block(n, plan, table, pulled):
    total = None
    for k in range(KP):
        at = n * FIELDS + 3 * k
        left = dot(table[plan[at + 2]], pulled(plan[at + 1])).astype(BF16)
        term = lax.dot_general(
            left, table[plan[at + 3]], (((1,), (1,)), ((), ())), preferred_element_type=F32
        )
        total = term if total is None else total + term
    return total.astype(BF16)


def near_kernel(count, plan, source, table, begun):
    for n in range(count - CAP):
        begun[n] = warp_block(n, plan, table, lambda index: source[index])


def window(picture, y, x):
    top = pl.multiple_of(jnp.minimum(y // 16 * 16, picture.shape[0] - ROWS), 16)
    left = pl.multiple_of(jnp.minimum(x // PS * PS, picture.shape[1] - COLS), PS)
    area = picture[pl.ds(top, ROWS), pl.ds(left, COLS)]
    i = lax.broadcasted_iota(jnp.int32, (PS, ROWS), 0)
    r = lax.broadcasted_iota(jnp.int32, (PS, ROWS), 1)
    pick_rows = (r - i == y - top).astype(F32).astype(BF16)
    c = lax.broadcasted_iota(jnp.int32, (COLS, PS), 0)
    j = lax.broadcasted_iota(jnp.int32, (COLS, PS), 1)
    pick_cols = (c - j == x - left).astype(F32).astype(BF16)
    return dot(dot(pick_rows, area).astype(BF16), pick_cols).astype(BF16)


def cut_windows(share, corners, picture, out):
    for n, p in enumerate(share):
        out[n] = window(picture, corners[0, p], corners[1, p])


def far_kernel(count, grid, share, plan, corners, source, other, table, begun, picture, out):
    near = count - CAP

    def pulled(index):
        here = index < count
        own = source[jnp.where(here, index, 0)]
        return jnp.where(here, own, other[jnp.where(here, 0, index - count)])

    for n in range(near):
        picture[place(plan[n * FIELDS], grid)] = begun[n]
    for n in range(near, count):
        picture[place(plan[n * FIELDS], grid)] = warp_block(n, plan, table, pulled)
    cut_windows(share, corners, picture, out)


def spectrum_columns(patch, forward, constant):
    values = patch.astype(F32)
    mean = jnp.sum(values, keepdims=True) * (1.0 / (PS * PS))
    centred = values - mean
    power = jnp.sum(centred * centred, keepdims=True) * (1.0 / (PS * PS))
    halves = dot(jnp.concatenate([patch, patch], axis=1), forward[...]) - mean * constant[...]
    halves = halves.astype(BF16)
    return halves[:, :PS], halves[:, PS:], power


def own_kernel(patches, corners, picture, forward, constant, down, out, power_out, warped, bands, halves, sem):
    write = pltpu.make_async_copy(picture, warped, sem)
    write.start()
    cut_windows(range(patches), corners, picture, bands)
    for p in range(patches):
        cosine_part, sine_part, power = spectrum_columns(bands[p], forward, constant)
        halves[p, :PS] = cosine_part
        halves[p, PS:] = sine_part
        power_out[pl.ds(p, 1), :] = jnp.broadcast_to(power, (1, PS))
    for p in range(patches):
        out[p] = dot(down[...], halves[p])
    write.wait()


def match_kernel(
    share, previous, spectra, powers, forward, constant, down, back, *rest
):
    out, halves, crosses, mixed, scales, done, sems = rest[-7:]
    pairs = [share[start : start + 2] for start in range(0, len(share), 2)]
    for n, p in enumerate(share):
        cosine_part, sine_part, power = spectrum_columns(previous[n], forward, constant)
        at = pl.ds(n % 2 * PS, PS)
        halves[n // 2, :PS, at] = cosine_part
        halves[n // 2, PS:, at] = sine_part
        product = (powers[pl.ds(p, 1), :] + EPSILON) * (power + EPSILON)
        scales[pl.ds(n, 1), :] = lax.rsqrt(product) * (1.0 / (PS * PS * PS))
    for q, pair in enumerate(pairs):
        width = PS * len(pair)
        second = dot(down[...], halves[q, :, :width])
        for n, p in enumerate(pair):
            one_real, one_imag = spectra[p, :PS, :], spectra[p, PS:, :]
            two_real, two_imag = second[:PS, n * PS : (n + 1) * PS], second[PS:, n * PS : (n + 1) * PS]
            real = one_real * two_real + one_imag * two_imag
            imag = one_real * two_imag - one_imag * two_real
            crosses[q, :PS, pl.ds(n * PS, PS)] = real.astype(BF16)
            crosses[q, PS:, pl.ds(n * PS, PS)] = imag.astype(BF16)
    for q, pair in enumerate(pairs):
        width = PS * len(pair)
        both = dot(down[...], crosses[q, :, :width]).astype(BF16)
        for n, p in enumerate(pair):
            mixed[2 * q + n, :, :PS] = both[:PS, n * PS : (n + 1) * PS]
            mixed[2 * q + n, :, PS:] = both[PS:, n * PS : (n + 1) * PS]
    writes = []
    group = 5
    for n, p in enumerate(share):
        done[n] = dot(mixed[n], back[...]) * scales[pl.ds(n, 1), :]
        if n % group == group - 1 or n == len(share) - 1:
            first = n // group * group
            size = n + 1 - first
            writes.append(
                pltpu.make_async_copy(
                    done.at[pl.ds(first, size)],
                    out.at[pl.ds(share[0] + first, size)],
                    sems.at[n // group],
                )
            )
            writes[-1].start()
    for write in writes:
        write.wait()


def shares_of(patches):
    cuts = [0] + [round(patches * part) for part in PARTS] + [patches]
    return [range(a, b) for a, b in zip(cuts, cuts[1:])]


def params(megabytes, flops, moved):
    return dict(
        compiler_params=pltpu.CompilerParams(vmem_limit_bytes=megabytes << 20),
        cost_estimate=pl.CostEstimate(flops=flops, bytes_accessed=moved, transcendentals=0),
    )


def shards(source, pull_ids, interp_idx, interp_table, patch_pos):
    blocks = source[0]
    count = blocks.shape[0]
    grid = int(round(count**0.5))
    patches = patch_pos.shape[1]
    side = grid * BS
    near = count - CAP
    ids = pull_ids.transpose(2, 0, 1)
    mats = interp_idx[0].transpose(1, 2, 0)
    positions = patch_pos[0].T
    shares = shares_of(patches)
    sections = lax.axis_size("sec")
    tiles = lax.axis_size("tile")
    other = lax.ppermute(blocks, "tile", [(i, (i + 1) % tiles) for i in range(tiles)])
    plan = pl.pallas_call(
        functools.partial(plan_kernel, count, tiles),
        out_shape=jax.ShapeDtypeStruct((count * FIELDS,), jnp.int32),
        in_specs=[ANY] * 2,
        out_specs=SMEM,
        scratch_shapes=[
            pltpu.SMEM(ids.shape, jnp.int32),
            pltpu.SMEM(mats.shape, jnp.int32),
            pltpu.SemaphoreType.DMA((3,)),
        ],
        **params(16, 2 << 30, 16 << 20),
    )(ids, mats)
    plan, asked = lax.optimization_barrier((plan, positions))
    wanted = lax.ppermute(asked, "sec", [(i + 1, i) for i in range(sections - 1)])
    forward, constant, down, back = tables()

    begun = pl.pallas_call(
        functools.partial(near_kernel, count),
        out_shape=jax.ShapeDtypeStruct((near, BS, BS), BF16),
        in_specs=[SMEM, VMEM, VMEM],
        out_specs=VMEM,
        **params(16, near * KP * 4 * BS**3, near * (KP + 1) * BS * BS * 2),
    )(plan, blocks, interp_table)

    picture, sent = pl.pallas_call(
        functools.partial(far_kernel, count, grid, shares[0]),
        out_shape=(
            jax.ShapeDtypeStruct((side, side), BF16),
            jax.ShapeDtypeStruct((len(shares[0]), PS, PS), BF16),
        ),
        in_specs=[SMEM] * 2 + [VMEM] * 4,
        out_specs=(VMEM, VMEM),
        **params(16, CAP * KP * 4 * BS**3, CAP * (KP + 1) * BS * BS * 2),
    )(plan, wanted, blocks, other, interp_table, begun)

    onward = [(i, i + 1) for i in range(sections - 1)]
    arrivals = [lax.ppermute(sent, "sec", onward)]
    for share in shares[1:]:
        sent = pl.pallas_call(
            functools.partial(cut_windows, share),
            out_shape=jax.ShapeDtypeStruct((len(share), PS, PS), BF16),
            in_specs=[SMEM, VMEM],
            out_specs=VMEM,
            **params(16, len(share) * 10 * PS**3, len(share) * PS * PS * 8),
        )(wanted, picture)
        arrivals.append(lax.ppermute(sent, "sec", onward))

    spectra, powers, warped = pl.pallas_call(
        functools.partial(own_kernel, patches),
        out_shape=(
            jax.ShapeDtypeStruct((patches, 2 * PS, PS), F32),
            jax.ShapeDtypeStruct((patches, PS), F32),
            jax.ShapeDtypeStruct((side, side), BF16),
        ),
        in_specs=[SMEM] + [VMEM] * 4,
        out_specs=(VMEM, VMEM, ANY),
        scratch_shapes=[
            pltpu.VMEM((patches, PS, PS), BF16),
            pltpu.VMEM((patches, 2 * PS, PS), BF16),
            pltpu.SemaphoreType.DMA,
        ],
        **params(20, patches * 12 * PS**3, side * side * 2),
    )(positions, picture, forward, constant, down)

    correlations = ()
    for share, previous in zip(shares, arrivals):
        size = len(share)
        correlations = (
            pl.pallas_call(
                functools.partial(match_kernel, share),
                out_shape=jax.ShapeDtypeStruct((patches, PS, PS), F32),
                in_specs=[VMEM] * 7 + [ANY] * len(correlations),
                out_specs=ANY,
                scratch_shapes=[
                    pltpu.VMEM(((size + 1) // 2, 2 * PS, 2 * PS), BF16),
                    pltpu.VMEM(((size + 1) // 2, 2 * PS, 2 * PS), BF16),
                    pltpu.VMEM((size, PS, 2 * PS), BF16),
                    pltpu.VMEM((size, PS), F32),
                    pltpu.VMEM((size, PS, PS), F32),
                    pltpu.SemaphoreType.DMA(((size + 4) // 5,)),
                ],
                input_output_aliases={7: 0} if correlations else {},
                **params(16, size * 16 * PS**3, size * PS * PS * 14),
            )(previous, spectra, powers, forward, constant, down, back, *correlations),
        )
    (correlations,) = correlations
    return warped[None], correlations[None]


def solution(mesh):
    return jax.shard_map(
        shards,
        mesh=mesh,
        in_specs=(
            P(("parts", "sec"), "tile", None, None),
            P(("parts", "sec"), "tile", None),
            P(("parts", "sec"), "tile", None, None),
            P(),
            P(("parts", "sec"), "tile", None),
        ),
        out_specs=(P(("parts", "sec"), "tile", None), P(("parts", "sec"), "tile", None, None)),
        check_vma=False,
    )
```

```python
import functools

import jax
import jax.numpy as jnp
import ml_dtypes
import numpy as np
from jax import lax
from jax.experimental import pallas as pl
from jax.experimental.pallas import tpu as pltpu
from jax.sharding import PartitionSpec as P

BS = 256
PS = 128
KP = 3
EPSILON = 1e-06
CAP = 12
ROWS = PS + 16
COLS = 2 * PS
PARTS = (0.64,)

SMEM = pl.BlockSpec(memory_space=pltpu.SMEM)
VMEM = pl.BlockSpec(memory_space=pltpu.VMEM)
ANY = pl.BlockSpec(memory_space=pl.ANY)
F32 = jnp.float32
BF16 = jnp.bfloat16


def tables():
    grid = np.arange(PS)
    folded = np.minimum(grid, PS - grid)
    quarter = np.minimum(folded, PS // 2 - folded)
    wave = np.sign(PS // 4 - folded) * np.cos(2.0 * np.pi / PS * quarter)
    phase = grid[:, None] * grid[None, :] % PS
    cosine, sine = wave[phase], wave[(phase + 3 * PS // 4) % PS]
    across = np.concatenate([cosine, sine], axis=1)
    high = across.astype(ml_dtypes.bfloat16)
    low = (across - high.astype(np.float64)).astype(ml_dtypes.bfloat16)
    forward = np.concatenate([high, low], axis=0)
    lowest = (grid[None, :] == 0).astype(np.float32) / PS
    down = np.block([[cosine, -sine], [sine, cosine]]).astype(ml_dtypes.bfloat16)
    back = np.concatenate([cosine, -sine], axis=0).astype(ml_dtypes.bfloat16)
    return forward, lowest, down, back


def dot(a, b):
    return jnp.dot(a, b, preferred_element_type=F32)


FIELDS = 1 + 3 * KP


def gate_kernel(out):
    out[...] = jnp.zeros(out.shape, out.dtype)


def make_plan(count, tiles, ids, mats, plan):
    low = lax.axis_index("tile") * count
    first, last = jnp.int32(0), jnp.int32(count - 1)
    for b in range(count):
        near, pulls = None, []
        for k in range(KP):
            local = ids[k, 0, b] - low
            here = (local >= 0) & (local < count)
            near = here if near is None else near & here
            pulls.append(jnp.where(local < 0, local + tiles * count, local))
        step = near.astype(jnp.int32)
        at = (last + step * (first - last)) * FIELDS
        first = first + step
        last = last + step - 1
        plan[at] = b
        for k in range(KP):
            plan[at + 1 + 3 * k] = pulls[k]
            plan[at + 2 + 3 * k] = mats[k, 0, b]
            plan[at + 3 + 3 * k] = mats[k, 1, b]


def place(block, grid):
    row = pl.multiple_of(block // grid * BS, BS)
    col = pl.multiple_of(block % grid * BS, BS)
    return pl.ds(row, BS), pl.ds(col, BS)


def warp_block(n, plan, table, pulled):
    total = None
    for k in range(KP):
        at = n * FIELDS + 3 * k
        left = dot(table[plan[at + 2]], pulled(plan[at + 1])).astype(BF16)
        term = lax.dot_general(
            left, table[plan[at + 3]], (((1,), (1,)), ((), ())), preferred_element_type=F32
        )
        total = term if total is None else total + term
    return total.astype(BF16)


def near_kernel(count, tiles, ids, mats, source, table, gate, begun, plan):
    make_plan(count, tiles, ids, mats, plan)
    for n in range(count - CAP):
        begun[n] = warp_block(n, plan, table, lambda index: source[index])


def window(picture, y, x):
    top = pl.multiple_of(jnp.minimum(y // 16 * 16, picture.shape[0] - ROWS), 16)
    left = pl.multiple_of(jnp.minimum(x // PS * PS, picture.shape[1] - COLS), PS)
    area = picture[pl.ds(top, ROWS), pl.ds(left, COLS)]
    i = lax.broadcasted_iota(jnp.int32, (PS, ROWS), 0)
    r = lax.broadcasted_iota(jnp.int32, (PS, ROWS), 1)
    pick_rows = (r - i == y - top).astype(F32).astype(BF16)
    c = lax.broadcasted_iota(jnp.int32, (COLS, PS), 0)
    j = lax.broadcasted_iota(jnp.int32, (COLS, PS), 1)
    pick_cols = (c - j == x - left).astype(F32).astype(BF16)
    return dot(dot(pick_rows, area).astype(BF16), pick_cols).astype(BF16)


def cut_windows(share, corners, picture, out):
    for n, p in enumerate(share):
        out[n] = window(picture, corners[0, p], corners[1, p])


def far_kernel(
    count, tiles, grid, share, ids, mats, corners, source, other, table, begun, picture, out, plan
):
    near = count - CAP
    make_plan(count, tiles, ids, mats, plan)

    def pulled(index):
        here = index < count
        own = source[jnp.where(here, index, 0)]
        return jnp.where(here, own, other[jnp.where(here, 0, index - count)])

    for n in range(near):
        picture[place(plan[n * FIELDS], grid)] = begun[n]
    for n in range(near, count):
        picture[place(plan[n * FIELDS], grid)] = warp_block(n, plan, table, pulled)
    cut_windows(share, corners, picture, out)


def spectrum_columns(patch, forward, lowest):
    halves = dot(jnp.concatenate([patch, patch], axis=1), forward[...])
    cosine_part, sine_part = halves[:, :PS], halves[:, PS:]
    cosine_part = cosine_part - jnp.sum(cosine_part, axis=0, keepdims=True) * lowest[...]
    return cosine_part.astype(BF16), sine_part.astype(BF16)


def energy(real, imag):
    return jnp.sum(real * real + imag * imag, axis=0, keepdims=True)


def mean_square(energies):
    return jnp.sum(energies, axis=1, keepdims=True) * (1.0 / PS**4)


def own_kernel(patches, corners, picture, forward, lowest, down, out, power_out, warped, bands, halves, sem):
    write = pltpu.make_async_copy(picture, warped, sem)
    write.start()
    cut_windows(range(patches), corners, picture, bands)
    for p in range(patches):
        halves[p, :PS], halves[p, PS:] = spectrum_columns(bands[p], forward, lowest)
    for p in range(patches):
        both = dot(down[...], halves[p])
        out[p] = both
        power_out[pl.ds(p, 1), :] = energy(both[:PS], both[PS:])
    power_out[...] = jnp.broadcast_to(mean_square(power_out[...]), power_out.shape)
    write.wait()


def match_kernel(
    share, previous, spectra, powers, forward, lowest, down, back, *rest
):
    out, halves, crosses, mixed, scales, done, sems = rest[-7:]
    pairs = [share[start : start + 2] for start in range(0, len(share), 2)]
    for n in range(len(share)):
        at = pl.ds(n % 2 * PS, PS)
        halves[n // 2, :PS, at], halves[n // 2, PS:, at] = spectrum_columns(previous[n], forward, lowest)
    for q, pair in enumerate(pairs):
        width = PS * len(pair)
        second = dot(down[...], halves[q, :, :width])
        for n, p in enumerate(pair):
            one_real, one_imag = spectra[p, :PS, :], spectra[p, PS:, :]
            two_real, two_imag = second[:PS, n * PS : (n + 1) * PS], second[PS:, n * PS : (n + 1) * PS]
            scales[pl.ds(2 * q + n, 1), :] = energy(two_real, two_imag)
            real = one_real * two_real + one_imag * two_imag
            imag = one_real * two_imag - one_imag * two_real
            crosses[q, :PS, pl.ds(n * PS, PS)] = real.astype(BF16)
            crosses[q, PS:, pl.ds(n * PS, PS)] = imag.astype(BF16)
    for q, pair in enumerate(pairs):
        width = PS * len(pair)
        both = dot(down[...], crosses[q, :, :width]).astype(BF16)
        for n, p in enumerate(pair):
            mixed[2 * q + n, :, :PS] = both[:PS, n * PS : (n + 1) * PS]
            mixed[2 * q + n, :, PS:] = both[PS:, n * PS : (n + 1) * PS]
    product = (powers[pl.ds(share[0], len(share)), :] + EPSILON) * (mean_square(scales[...]) + EPSILON)
    scales[...] = lax.rsqrt(product) * (1.0 / (PS * PS * PS))
    writes = []
    group = 5
    for n in range(len(share)):
        done[n] = dot(mixed[n], back[...]) * scales[pl.ds(n, 1), :]
        if n % group == group - 1 or n == len(share) - 1:
            first = n // group * group
            size = n + 1 - first
            writes.append(
                pltpu.make_async_copy(
                    done.at[pl.ds(first, size)],
                    out.at[pl.ds(share[0] + first, size)],
                    sems.at[n // group],
                )
            )
            writes[-1].start()
    for write in writes:
        write.wait()


def shares_of(patches):
    cuts = [0] + [round(patches * part) for part in PARTS] + [patches]
    return [range(a, b) for a, b in zip(cuts, cuts[1:])]


def params(megabytes, flops, moved):
    return dict(
        compiler_params=pltpu.CompilerParams(vmem_limit_bytes=megabytes << 20),
        cost_estimate=pl.CostEstimate(flops=flops, bytes_accessed=moved, transcendentals=0),
    )


def shards(source, pull_ids, interp_idx, interp_table, patch_pos):
    blocks = source[0]
    count = blocks.shape[0]
    grid = int(round(count**0.5))
    patches = patch_pos.shape[1]
    side = grid * BS
    near = count - CAP
    ids = pull_ids.transpose(2, 0, 1)
    mats = interp_idx[0].transpose(1, 2, 0)
    positions = patch_pos[0].T
    shares = shares_of(patches)
    sections = lax.axis_size("sec")
    tiles = lax.axis_size("tile")
    other = lax.ppermute(blocks, "tile", [(i, (i + 1) % tiles) for i in range(tiles)])
    gate = pl.pallas_call(
        gate_kernel,
        out_shape=jax.ShapeDtypeStruct((8, 128), F32),
        out_specs=VMEM,
        **params(16, 2 << 30, 16 << 20),
    )()
    gate, asked = lax.optimization_barrier((gate, positions))
    wanted = lax.ppermute(asked, "sec", [(i + 1, i) for i in range(sections - 1)])
    forward, lowest, down, back = tables()

    begun = pl.pallas_call(
        functools.partial(near_kernel, count, tiles),
        out_shape=jax.ShapeDtypeStruct((near, BS, BS), BF16),
        in_specs=[SMEM, SMEM, VMEM, VMEM, ANY],
        out_specs=VMEM,
        scratch_shapes=[pltpu.SMEM((count * FIELDS,), jnp.int32)],
        **params(16, near * KP * 4 * BS**3, near * (KP + 1) * BS * BS * 2),
    )(ids, mats, blocks, interp_table, gate)

    picture, sent = pl.pallas_call(
        functools.partial(far_kernel, count, tiles, grid, shares[0]),
        out_shape=(
            jax.ShapeDtypeStruct((side, side), BF16),
            jax.ShapeDtypeStruct((len(shares[0]), PS, PS), BF16),
        ),
        in_specs=[SMEM] * 3 + [VMEM] * 4,
        out_specs=(VMEM, VMEM),
        scratch_shapes=[pltpu.SMEM((count * FIELDS,), jnp.int32)],
        **params(16, CAP * KP * 4 * BS**3, CAP * (KP + 1) * BS * BS * 2),
    )(ids, mats, wanted, blocks, other, interp_table, begun)

    onward = [(i, i + 1) for i in range(sections - 1)]
    arrivals = [lax.ppermute(sent, "sec", onward)]
    for share in shares[1:]:
        sent = pl.pallas_call(
            functools.partial(cut_windows, share),
            out_shape=jax.ShapeDtypeStruct((len(share), PS, PS), BF16),
            in_specs=[SMEM, VMEM],
            out_specs=VMEM,
            **params(16, len(share) * 10 * PS**3, len(share) * PS * PS * 8),
        )(wanted, picture)
        arrivals.append(lax.ppermute(sent, "sec", onward))

    spectra, powers, warped = pl.pallas_call(
        functools.partial(own_kernel, patches),
        out_shape=(
            jax.ShapeDtypeStruct((patches, 2 * PS, PS), F32),
            jax.ShapeDtypeStruct((patches, PS), F32),
            jax.ShapeDtypeStruct((side, side), BF16),
        ),
        in_specs=[SMEM] + [VMEM] * 4,
        out_specs=(VMEM, VMEM, ANY),
        scratch_shapes=[
            pltpu.VMEM((patches, PS, PS), BF16),
            pltpu.VMEM((patches, 2 * PS, PS), BF16),
            pltpu.SemaphoreType.DMA,
        ],
        **params(20, patches * 12 * PS**3, side * side * 2),
    )(positions, picture, forward, lowest, down)

    correlations = ()
    for share, previous in zip(shares, arrivals):
        size = len(share)
        correlations = (
            pl.pallas_call(
                functools.partial(match_kernel, share),
                out_shape=jax.ShapeDtypeStruct((patches, PS, PS), F32),
                in_specs=[VMEM] * 7 + [ANY] * len(correlations),
                out_specs=ANY,
                scratch_shapes=[
                    pltpu.VMEM(((size + 1) // 2, 2 * PS, 2 * PS), BF16),
                    pltpu.VMEM(((size + 1) // 2, 2 * PS, 2 * PS), BF16),
                    pltpu.VMEM((size, PS, 2 * PS), BF16),
                    pltpu.VMEM((size, PS), F32),
                    pltpu.VMEM((size, PS, PS), F32),
                    pltpu.SemaphoreType.DMA(((size + 4) // 5,)),
                ],
                input_output_aliases={7: 0} if correlations else {},
                **params(16, size * 16 * PS**3, size * PS * PS * 14),
            )(previous, spectra, powers, forward, lowest, down, back, *correlations),
        )
    (correlations,) = correlations
    return warped[None], correlations[None]


def solution(mesh):
    return jax.shard_map(
        shards,
        mesh=mesh,
        in_specs=(
            P(("parts", "sec"), "tile", None, None),
            P(("parts", "sec"), "tile", None),
            P(("parts", "sec"), "tile", None, None),
            P(),
            P(("parts", "sec"), "tile", None),
        ),
        out_specs=(P(("parts", "sec"), "tile", None), P(("parts", "sec"), "tile", None, None)),
        check_vma=False,
    )
```

```python
import functools

import jax
import jax.numpy as jnp
import ml_dtypes
import numpy as np
from jax import lax
from jax.experimental import pallas as pl
from jax.experimental.pallas import tpu as pltpu
from jax.sharding import PartitionSpec as P

BS = 256
PS = 128
KP = 3
EPSILON = 1e-06
ROWS = PS + 16
COLS = 2 * PS

SMEM = pl.BlockSpec(memory_space=pltpu.SMEM)
VMEM = pl.BlockSpec(memory_space=pltpu.VMEM)
ANY = pl.BlockSpec(memory_space=pl.ANY)
F32 = jnp.float32
BF16 = jnp.bfloat16


def tables():
    grid = np.arange(PS)
    folded = np.minimum(grid, PS - grid)
    quarter = np.minimum(folded, PS // 2 - folded)
    wave = np.sign(PS // 4 - folded) * np.cos(2.0 * np.pi / PS * quarter)
    phase = grid[:, None] * grid[None, :] % PS
    cosine, sine = wave[phase], wave[(phase + 3 * PS // 4) % PS]
    across = np.concatenate([cosine, sine], axis=1)
    high = across.astype(ml_dtypes.bfloat16)
    low = (across - high.astype(np.float64)).astype(ml_dtypes.bfloat16)
    forward = np.concatenate([high, low], axis=0)
    lowest = (grid[None, :] == 0).astype(np.float32) / PS
    down = np.block([[cosine, -sine], [sine, cosine]]).astype(ml_dtypes.bfloat16)
    back = np.concatenate([cosine, -sine], axis=0).astype(ml_dtypes.bfloat16)
    return forward, lowest, down, back


def dot(a, b):
    return jnp.dot(a, b, preferred_element_type=F32)


def gate_kernel(out):
    out[...] = jnp.zeros(out.shape, out.dtype)


def early_rows(grid):
    return grid // 2 + 1


def from_top(corners, patches, grid):
    fitting = jnp.int32(0)
    for p in range(patches):
        fitting = fitting + (corners[0, p] <= early_rows(grid) * BS - PS).astype(jnp.int32)
    return fitting >= (patches + 1) // 2


def window_order(corners, order, patches, grid):
    down = jnp.where(from_top(corners, patches, grid), 0, grid - early_rows(grid))
    low = down * BS
    high = low + early_rows(grid) * BS - PS
    front, back = jnp.int32(0), jnp.int32(patches - 1)
    for p in range(patches):
        y = corners[0, p]
        early = ((y >= low) & (y <= high) & (front < (patches + 1) // 2)).astype(jnp.int32)
        order[back + early * (front - back)] = p
        front = front + early
        back = back + early - 1
    return down


def warp_block(block, low, count, ids, mats, source, other, table):
    total = None
    for k in range(KP):
        local = ids[k, 0, block] - low
        here = (local >= 0) & (local < count)
        away = jnp.where(local < 0, local + count, local - count)
        pulled = jnp.where(here, source[jnp.where(here, local, 0)], other[jnp.where(here, 0, away)])
        left = dot(table[mats[k, 0, block]], pulled).astype(BF16)
        term = lax.dot_general(
            left, table[mats[k, 1, block]], (((1,), (1,)), ((), ())), preferred_element_type=F32
        )
        total = term if total is None else total + term
    return total.astype(BF16)


def window(picture, y, x):
    top = pl.multiple_of(jnp.minimum(y // 16 * 16, picture.shape[0] - ROWS), 16)
    left = pl.multiple_of(jnp.minimum(x // PS * PS, picture.shape[1] - COLS), PS)
    area = picture[pl.ds(top, ROWS), pl.ds(left, COLS)]
    i = lax.broadcasted_iota(jnp.int32, (PS, ROWS), 0)
    r = lax.broadcasted_iota(jnp.int32, (PS, ROWS), 1)
    pick_rows = (r - i == y - top).astype(F32).astype(BF16)
    c = lax.broadcasted_iota(jnp.int32, (COLS, PS), 0)
    j = lax.broadcasted_iota(jnp.int32, (COLS, PS), 1)
    pick_cols = (c - j == x - left).astype(F32).astype(BF16)
    return dot(dot(pick_rows, area).astype(BF16), pick_cols).astype(BF16)


def early_kernel(
    count, grid, patches, ids, mats, corners, source, other, table, gate, early, out, order
):
    low = lax.axis_index("tile") * count
    down = window_order(corners, order, patches, grid)
    for n in range(early_rows(grid) * grid):
        block = down * grid + n
        at = pl.ds(n // grid * BS, BS), pl.ds(n % grid * BS, BS)
        early[at] = warp_block(block, low, count, ids, mats, source, other, table)
    for n in range(out.shape[0]):
        p = order[n]
        out[n] = window(early, corners[0, p] - down * BS, corners[1, p])


def late_kernel(
    count, grid, patches, ids, mats, corners, source, other, table, early, picture, out, order
):
    low = lax.axis_index("tile") * count
    rows = early_rows(grid)
    down = window_order(corners, order, patches, grid)
    for n in range(rows):
        picture[pl.ds(pl.multiple_of((down + n) * BS, BS), BS), :] = early[pl.ds(n * BS, BS), :]
    after = lax.rem(down + rows, grid)
    for n in range((grid - rows) * grid):
        row = pl.multiple_of((after + n // grid) * BS, BS)
        block = after * grid + n
        picture[pl.ds(row, BS), pl.ds(n % grid * BS, BS)] = warp_block(
            block, low, count, ids, mats, source, other, table
        )
    for n in range(out.shape[0]):
        p = order[patches - out.shape[0] + n]
        out[n] = window(picture, corners[0, p], corners[1, p])


def spectrum_columns(patch, forward, lowest):
    halves = dot(jnp.concatenate([patch, patch], axis=1), forward[...])
    cosine_part, sine_part = halves[:, :PS], halves[:, PS:]
    cosine_part = cosine_part - jnp.sum(cosine_part, axis=0, keepdims=True) * lowest[...]
    return cosine_part.astype(BF16), sine_part.astype(BF16)


def energy(real, imag):
    return jnp.sum(real * real + imag * imag, axis=0, keepdims=True)


def mean_square(energies):
    return jnp.sum(energies, axis=1, keepdims=True) * (1.0 / PS**4)


def own_kernel(
    patches, grid, corners, picture, forward, lowest, down, out, power_out, warped, order, bands, halves, sem
):
    write = pltpu.make_async_copy(picture, warped, sem)
    write.start()
    window_order(corners, order, patches, grid)
    for n in range(patches):
        p = order[n]
        bands[n] = window(picture, corners[0, p], corners[1, p])
    for p in range(patches):
        halves[p, :PS], halves[p, PS:] = spectrum_columns(bands[p], forward, lowest)
    for p in range(patches):
        both = dot(down[...], halves[p])
        out[p] = both
        power_out[pl.ds(p, 1), :] = energy(both[:PS], both[PS:])
    power_out[...] = jnp.broadcast_to(mean_square(power_out[...]), power_out.shape)
    write.wait()


def match_kernel(
    share, order, previous, spectra, powers, forward, lowest, down, back, *rest
):
    out, halves, crosses, mixed, scales, done, slots, sems, slots_sem = rest[-9:]
    fetch = pltpu.make_async_copy(order, slots, slots_sem)
    fetch.start()
    pairs = [share[start : start + 2] for start in range(0, len(share), 2)]
    for n in range(len(share)):
        at = pl.ds(n % 2 * PS, PS)
        halves[n // 2, :PS, at], halves[n // 2, PS:, at] = spectrum_columns(previous[n], forward, lowest)
    for q, pair in enumerate(pairs):
        width = PS * len(pair)
        second = dot(down[...], halves[q, :, :width])
        for n, p in enumerate(pair):
            one_real, one_imag = spectra[p, :PS, :], spectra[p, PS:, :]
            two_real, two_imag = second[:PS, n * PS : (n + 1) * PS], second[PS:, n * PS : (n + 1) * PS]
            scales[pl.ds(2 * q + n, 1), :] = energy(two_real, two_imag)
            real = one_real * two_real + one_imag * two_imag
            imag = one_real * two_imag - one_imag * two_real
            crosses[q, :PS, pl.ds(n * PS, PS)] = real.astype(BF16)
            crosses[q, PS:, pl.ds(n * PS, PS)] = imag.astype(BF16)
    for q, pair in enumerate(pairs):
        width = PS * len(pair)
        both = dot(down[...], crosses[q, :, :width]).astype(BF16)
        for n, p in enumerate(pair):
            mixed[2 * q + n, :, :PS] = both[:PS, n * PS : (n + 1) * PS]
            mixed[2 * q + n, :, PS:] = both[PS:, n * PS : (n + 1) * PS]
    product = (powers[pl.ds(share[0], len(share)), :] + EPSILON) * (mean_square(scales[...]) + EPSILON)
    scales[...] = lax.rsqrt(product) * (1.0 / (PS * PS * PS))
    fetch.wait()
    writes = []
    for n, p in enumerate(share):
        done[n] = dot(mixed[n], back[...]) * scales[pl.ds(n, 1), :]
        writes.append(pltpu.make_async_copy(done.at[n], out.at[slots[p]], sems.at[n]))
        writes[-1].start()
    for write in writes:
        write.wait()


def params(megabytes, flops, moved):
    return dict(
        compiler_params=pltpu.CompilerParams(vmem_limit_bytes=megabytes << 20),
        cost_estimate=pl.CostEstimate(flops=flops, bytes_accessed=moved, transcendentals=0),
    )


def shards(source, pull_ids, interp_idx, interp_table, patch_pos):
    blocks = source[0]
    count = blocks.shape[0]
    grid = int(round(count**0.5))
    patches = patch_pos.shape[1]
    side = grid * BS
    ids = pull_ids.transpose(2, 0, 1)
    mats = interp_idx[0].transpose(1, 2, 0)
    positions = patch_pos[0].T
    shares = range((patches + 1) // 2), range((patches + 1) // 2, patches)
    sections = lax.axis_size("sec")
    tiles = lax.axis_size("tile")
    other = lax.ppermute(blocks, "tile", [(i, (i + 1) % tiles) for i in range(tiles)])
    gate = pl.pallas_call(
        gate_kernel,
        out_shape=jax.ShapeDtypeStruct((8, 128), F32),
        out_specs=VMEM,
        **params(16, 2 << 30, 16 << 20),
    )()
    gate, asked = lax.optimization_barrier((gate, positions))
    wanted = lax.ppermute(asked, "sec", [(i + 1, i) for i in range(sections - 1)])
    forward, lowest, down, back = tables()

    onward = [(i, i + 1) for i in range(sections - 1)]

    def warp_and_cut(kernel, share, blocks_made, shape, last):
        return pl.pallas_call(
            functools.partial(kernel, count, grid, patches),
            out_shape=(
                jax.ShapeDtypeStruct(shape, BF16),
                jax.ShapeDtypeStruct((len(share), PS, PS), BF16),
            ),
            in_specs=[SMEM] * 3 + [VMEM] * 3 + [ANY if kernel is early_kernel else VMEM],
            out_specs=(VMEM, VMEM),
            scratch_shapes=[pltpu.SMEM((patches,), jnp.int32)],
            **params(16, blocks_made * KP * 4 * BS**3, blocks_made * (KP + 1) * BS * BS * 2),
        )(ids, mats, wanted, blocks, other, interp_table, last)

    rows = early_rows(grid)
    early, sent = warp_and_cut(early_kernel, shares[0], rows * grid, (rows * BS, side), gate)
    arrivals = [lax.ppermute(sent, "sec", onward)]
    picture, sent = warp_and_cut(late_kernel, shares[1], (grid - rows) * grid, (side, side), early)
    arrivals.append(lax.ppermute(sent, "sec", onward))

    spectra, powers, warped, order = pl.pallas_call(
        functools.partial(own_kernel, patches, grid),
        out_shape=(
            jax.ShapeDtypeStruct((patches, 2 * PS, PS), F32),
            jax.ShapeDtypeStruct((patches, PS), F32),
            jax.ShapeDtypeStruct((side, side), BF16),
            jax.ShapeDtypeStruct((patches,), jnp.int32),
        ),
        in_specs=[SMEM] + [VMEM] * 4,
        out_specs=(VMEM, VMEM, ANY, SMEM),
        scratch_shapes=[
            pltpu.VMEM((patches, PS, PS), BF16),
            pltpu.VMEM((patches, 2 * PS, PS), BF16),
            pltpu.SemaphoreType.DMA,
        ],
        **params(20, patches * 12 * PS**3, side * side * 2),
    )(positions, picture, forward, lowest, down)

    correlations = ()
    for share, previous in zip(shares, arrivals):
        size = len(share)
        correlations = (
            pl.pallas_call(
                functools.partial(match_kernel, share),
                out_shape=jax.ShapeDtypeStruct((patches, PS, PS), F32),
                in_specs=[ANY] + [VMEM] * 7 + [ANY] * len(correlations),
                out_specs=ANY,
                scratch_shapes=[
                    pltpu.VMEM(((size + 1) // 2, 2 * PS, 2 * PS), BF16),
                    pltpu.VMEM(((size + 1) // 2, 2 * PS, 2 * PS), BF16),
                    pltpu.VMEM((size, PS, 2 * PS), BF16),
                    pltpu.VMEM((size, PS), F32),
                    pltpu.VMEM((size, PS, PS), F32),
                    pltpu.SMEM((patches,), jnp.int32),
                    pltpu.SemaphoreType.DMA((size,)),
                    pltpu.SemaphoreType.DMA,
                ],
                input_output_aliases={8: 0} if correlations else {},
                **params(16, size * 16 * PS**3, size * PS * PS * 14),
            )(order, previous, spectra, powers, forward, lowest, down, back, *correlations),
        )
    (correlations,) = correlations
    return warped[None], correlations[None]


def solution(mesh):
    return jax.shard_map(
        shards,
        mesh=mesh,
        in_specs=(
            P(("parts", "sec"), "tile", None, None),
            P(("parts", "sec"), "tile", None),
            P(("parts", "sec"), "tile", None, None),
            P(),
            P(("parts", "sec"), "tile", None),
        ),
        out_specs=(P(("parts", "sec"), "tile", None), P(("parts", "sec"), "tile", None, None)),
        check_vma=False,
    )
```

```python
import functools

import jax
import jax.numpy as jnp
import ml_dtypes
import numpy as np
from jax import lax
from jax.experimental import pallas as pl
from jax.experimental.pallas import tpu as pltpu
from jax.sharding import PartitionSpec as P

BS = 256
PS = 128
KP = 3
CAP = 12
LISTED = CAP + 1
EPSILON = 1e-06
ROWS = PS + 16
COLS = 2 * PS

SMEM = pl.BlockSpec(memory_space=pltpu.SMEM)
VMEM = pl.BlockSpec(memory_space=pltpu.VMEM)
ANY = pl.BlockSpec(memory_space=pl.ANY)
F32 = jnp.float32
BF16 = jnp.bfloat16


def tables():
    grid = np.arange(PS)
    folded = np.minimum(grid, PS - grid)
    quarter = np.minimum(folded, PS // 2 - folded)
    wave = np.sign(PS // 4 - folded) * np.cos(2.0 * np.pi / PS * quarter)
    phase = grid[:, None] * grid[None, :] % PS
    cosine, sine = wave[phase], wave[(phase + 3 * PS // 4) % PS]
    across = np.concatenate([cosine, sine], axis=1)
    high = across.astype(ml_dtypes.bfloat16)
    low = (across - high.astype(np.float64)).astype(ml_dtypes.bfloat16)
    forward = np.concatenate([high, low], axis=0)
    lowest = (grid[None, :] == 0).astype(np.float32) / PS
    down = np.block([[cosine, -sine], [sine, cosine]]).astype(ml_dtypes.bfloat16)
    back = np.concatenate([cosine, -sine], axis=0).astype(ml_dtypes.bfloat16)
    return forward, lowest, down, back


def dot(a, b):
    return jnp.dot(a, b, preferred_element_type=F32)


def gate_kernel(out):
    out[...] = jnp.zeros(out.shape, out.dtype)


def early_rows(grid):
    return grid // 2 + 1


def from_top(corners, patches, grid):
    fitting = jnp.int32(0)
    for p in range(patches):
        fitting = fitting + (corners[0, p] <= early_rows(grid) * BS - PS).astype(jnp.int32)
    return fitting >= (patches + 1) // 2


def window_order(corners, order, patches, grid):
    down = jnp.where(from_top(corners, patches, grid), 0, grid - early_rows(grid))
    low = down * BS
    high = low + early_rows(grid) * BS - PS
    front, back = jnp.int32(0), jnp.int32(patches - 1)
    for p in range(patches):
        y = corners[0, p]
        early = ((y >= low) & (y <= high) & (front < (patches + 1) // 2)).astype(jnp.int32)
        order[back + early * (front - back)] = p
        front = front + early
        back = back + early - 1
    return down


def near_kernel(count, grid, ids, mats, source, table, gate, lefts, plan):
    low = lax.axis_index("tile") * count
    pulls = count * KP
    for r in range(2 * LISTED):
        plan[pulls + r] = 0
    found = jnp.int32(0)
    for block in range(count):
        for k in range(KP):
            local = ids[k, 0, block] - low
            here = (local >= 0) & (local < count)
            plan[block * KP + k] = jnp.where(here, -1, found)
            slot = jnp.minimum(found, CAP)
            plan[pulls + slot] = jnp.where(here, 0, jnp.where(local < 0, local + count, local - count))
            plan[pulls + LISTED + slot] = mats[k, 0, block]
            found = found + jnp.where(here, 0, 1)
            if grid <= block < count - grid:
                left = dot(table[mats[k, 0, block]], source[jnp.where(here, local, 0)])
                lefts[(block - grid) * KP + k] = left.astype(BF16)


def warp_row(row, inner, low, grid, ids, mats, source, table, plan, lefts, others):
    blocks = []
    for column in range(grid):
        block = row * grid + column
        total = None
        for k in range(KP):
            slot = plan[block * KP + k]
            if inner:
                near = lefts[(block - grid) * KP + k]
            else:
                local = jnp.where(slot < 0, ids[k, 0, block] - low, 0)
                near = dot(table[mats[k, 0, block]], source[local]).astype(BF16)
            left = jnp.where(slot < 0, near, others[jnp.maximum(slot, 0)])
            term = lax.dot_general(
                left, table[mats[k, 1, block]], (((1,), (1,)), ((), ())), preferred_element_type=F32
            )
            total = term if total is None else total + term
        blocks.append(total.astype(BF16))
    return blocks


def cut_windows(picture, corners, wanted, above, bands, out):
    i = lax.broadcasted_iota(jnp.int32, (PS, ROWS), 0)
    r = lax.broadcasted_iota(jnp.int32, (PS, ROWS), 1)
    c = lax.broadcasted_iota(jnp.int32, (COLS, PS), 0)
    j = lax.broadcasted_iota(jnp.int32, (COLS, PS), 1)
    rests = []
    for n, p in enumerate(wanted):
        y, x = corners[0, p] - above, corners[1, p]
        top = pl.multiple_of(jnp.minimum(y // 16 * 16, picture.shape[0] - ROWS), 16)
        left = pl.multiple_of(jnp.minimum(x // PS * PS, picture.shape[1] - COLS), PS)
        pick_rows = (r - i == y - top).astype(F32).astype(BF16)
        bands[n] = dot(pick_rows, picture[pl.ds(top, ROWS), pl.ds(left, COLS)]).astype(BF16)
        rests.append(x - left)
    for n, rest in enumerate(rests):
        pick_cols = (c - j == rest).astype(F32).astype(BF16)
        out[n] = dot(bands[n], pick_cols).astype(BF16)


def fill_row(picture, row, blocks):
    for column, block in enumerate(blocks):
        picture[pl.ds(pl.multiple_of(row * BS, BS), BS), pl.ds(column * BS, BS)] = block


def early_kernel(
    grid, patches, plan, ids, mats, corners, source, other, table, lefts, early, others, out, order, bands
):
    pulls = grid * grid * KP
    low = lax.axis_index("tile") * grid * grid
    for r in range(CAP):
        left = dot(table[plan[pulls + LISTED + r]], other[plan[pulls + r]])
        others[r] = left.astype(BF16)
    down = window_order(corners, order, patches, grid)
    above = jnp.where(down == 0, 1, 0)
    given = ids, mats, source, table, plan, lefts, others
    for n in range(early_rows(grid) - 1):
        fill_row(early, n + above, warp_row(down + n + above, True, low, grid, *given))
    outer = jnp.where(down == 0, 0, grid - 1)
    fill_row(early, outer - down, warp_row(outer, False, low, grid, *given))
    cut_windows(early, corners, [order[n] for n in range(out.shape[0])], down * BS, bands, out)


def late_kernel(
    grid, patches, plan, ids, mats, corners, source, table, lefts, others, early, picture, out, order, bands
):
    rows = early_rows(grid)
    low = lax.axis_index("tile") * grid * grid
    down = window_order(corners, order, patches, grid)
    given = ids, mats, source, table, plan, lefts, others
    for n in range(rows):
        picture[pl.ds(pl.multiple_of((down + n) * BS, BS), BS), :] = early[pl.ds(n * BS, BS), :]
    for n in range(grid - rows - 1):
        row = jnp.where(down == 0, rows + n, 1 + n)
        fill_row(picture, row, warp_row(row, True, low, grid, *given))
    outer = jnp.where(down == 0, grid - 1, 0)
    fill_row(picture, outer, warp_row(outer, False, low, grid, *given))
    wanted = [order[n] for n in range(patches - out.shape[0], patches)]
    cut_windows(picture, corners, wanted, 0, bands, out)


def spectrum_columns(patch, forward, lowest):
    halves = dot(jnp.concatenate([patch, patch], axis=1), forward[...])
    cosine_part, sine_part = halves[:, :PS], halves[:, PS:]
    cosine_part = cosine_part - jnp.sum(cosine_part, axis=0, keepdims=True) * lowest[...]
    return cosine_part.astype(BF16), sine_part.astype(BF16)


def energy(real, imag):
    return jnp.sum(real * real + imag * imag, axis=0, keepdims=True)


def mean_square(energies):
    return jnp.sum(energies, axis=1, keepdims=True) * (1.0 / PS**4)


def own_kernel(
    patches, grid, corners, picture, forward, lowest, down, out, power_out, warped, order, rows, bands, halves, sem
):
    write = pltpu.make_async_copy(picture, warped, sem)
    write.start()
    window_order(corners, order, patches, grid)
    cut_windows(picture, corners, [order[n] for n in range(patches)], 0, rows, bands)
    for p in range(patches):
        halves[p, :PS], halves[p, PS:] = spectrum_columns(bands[p], forward, lowest)
    for p in range(patches):
        both = dot(down[...], halves[p])
        out[p] = both
        power_out[pl.ds(p, 1), :] = energy(both[:PS], both[PS:])
    power_out[...] = jnp.broadcast_to(mean_square(power_out[...]), power_out.shape)
    write.wait()


def match_kernel(
    share, order, previous, spectra, powers, forward, lowest, down, back, *rest
):
    out, halves, crosses, mixed, scales, done, slots, sems, slots_sem = rest[-9:]
    fetch = pltpu.make_async_copy(order, slots, slots_sem)
    fetch.start()
    pairs = [share[start : start + 2] for start in range(0, len(share), 2)]
    for n in range(len(share)):
        at = pl.ds(n % 2 * PS, PS)
        halves[n // 2, :PS, at], halves[n // 2, PS:, at] = spectrum_columns(previous[n], forward, lowest)
    for q, pair in enumerate(pairs):
        width = PS * len(pair)
        second = dot(down[...], halves[q, :, :width])
        for n, p in enumerate(pair):
            one_real, one_imag = spectra[p, :PS, :], spectra[p, PS:, :]
            two_real, two_imag = second[:PS, n * PS : (n + 1) * PS], second[PS:, n * PS : (n + 1) * PS]
            scales[pl.ds(2 * q + n, 1), :] = energy(two_real, two_imag)
            real = one_real * two_real + one_imag * two_imag
            imag = one_real * two_imag - one_imag * two_real
            crosses[q, :PS, pl.ds(n * PS, PS)] = real.astype(BF16)
            crosses[q, PS:, pl.ds(n * PS, PS)] = imag.astype(BF16)
    product = (powers[pl.ds(share[0], len(share)), :] + EPSILON) * (mean_square(scales[...]) + EPSILON)
    scales[...] = lax.rsqrt(product) * (1.0 / (PS * PS * PS))
    for q, pair in enumerate(pairs):
        width = PS * len(pair)
        both = dot(down[...], crosses[q, :, :width]).astype(BF16)
        for n, p in enumerate(pair):
            mixed[2 * q + n, :, :PS] = both[:PS, n * PS : (n + 1) * PS]
            mixed[2 * q + n, :, PS:] = both[PS:, n * PS : (n + 1) * PS]
    fetch.wait()
    writes = []
    for n, p in enumerate(share):
        done[n] = dot(mixed[n], back[...]) * scales[pl.ds(n, 1), :]
        writes.append(pltpu.make_async_copy(done.at[n], out.at[slots[p]], sems.at[n]))
        writes[-1].start()
    for write in writes:
        write.wait()


def params(megabytes, flops, moved):
    return dict(
        compiler_params=pltpu.CompilerParams(vmem_limit_bytes=megabytes << 20),
        cost_estimate=pl.CostEstimate(flops=flops, bytes_accessed=moved, transcendentals=0),
    )


def shards(source, pull_ids, interp_idx, interp_table, patch_pos):
    blocks = source[0]
    count = blocks.shape[0]
    grid = int(round(count**0.5))
    patches = patch_pos.shape[1]
    side = grid * BS
    ids = pull_ids.transpose(2, 0, 1)
    mats = interp_idx[0].transpose(1, 2, 0)
    positions = patch_pos[0].T
    shares = range((patches + 1) // 2), range((patches + 1) // 2, patches)
    sections = lax.axis_size("sec")
    tiles = lax.axis_size("tile")
    other = lax.ppermute(blocks, "tile", [(i, (i + 1) % tiles) for i in range(tiles)])
    gate = pl.pallas_call(
        gate_kernel,
        out_shape=jax.ShapeDtypeStruct((8, 128), F32),
        out_specs=VMEM,
        **params(16, 2 << 30, 16 << 20),
    )()
    gate, asked = lax.optimization_barrier((gate, positions))
    wanted = lax.ppermute(asked, "sec", [(i + 1, i) for i in range(sections - 1)])
    forward, lowest, down, back = tables()

    onward = [(i, i + 1) for i in range(sections - 1)]

    pulls = count * KP
    inner = pulls - 2 * grid * KP
    lefts, plan = pl.pallas_call(
        functools.partial(near_kernel, count, grid),
        out_shape=(
            jax.ShapeDtypeStruct((inner, BS, BS), BF16),
            jax.ShapeDtypeStruct((pulls + 2 * LISTED,), jnp.int32),
        ),
        in_specs=[SMEM, SMEM, VMEM, VMEM, ANY],
        out_specs=(VMEM, SMEM),
        **params(16, inner * 2 * BS**3, (count + inner) * BS * BS * 2),
    )(ids, mats, blocks, interp_table, gate)

    rows = early_rows(grid)
    early, others, sent = pl.pallas_call(
        functools.partial(early_kernel, grid, patches),
        out_shape=(
            jax.ShapeDtypeStruct((rows * BS, side), BF16),
            jax.ShapeDtypeStruct((CAP, BS, BS), BF16),
            jax.ShapeDtypeStruct((len(shares[0]), PS, PS), BF16),
        ),
        in_specs=[SMEM] * 4 + [VMEM] * 4,
        out_specs=[VMEM] * 3,
        scratch_shapes=[pltpu.SMEM((patches,), jnp.int32), pltpu.VMEM((len(shares[0]), PS, COLS), BF16)],
        **params(16, rows * grid * KP * 2 * BS**3, rows * grid * KP * BS * BS * 4),
    )(plan, ids, mats, wanted, blocks, other, interp_table, lefts)
    arrivals = [lax.ppermute(sent, "sec", onward)]
    picture, sent = pl.pallas_call(
        functools.partial(late_kernel, grid, patches),
        out_shape=(
            jax.ShapeDtypeStruct((side, side), BF16),
            jax.ShapeDtypeStruct((len(shares[1]), PS, PS), BF16),
        ),
        in_specs=[SMEM] * 4 + [VMEM] * 5,
        out_specs=[VMEM] * 2,
        scratch_shapes=[pltpu.SMEM((patches,), jnp.int32), pltpu.VMEM((len(shares[0]), PS, COLS), BF16)],
        **params(16, (grid - rows) * grid * KP * 2 * BS**3, side * side * 4),
    )(plan, ids, mats, wanted, blocks, interp_table, lefts, others, early)
    arrivals.append(lax.ppermute(sent, "sec", onward))

    spectra, powers, warped, order = pl.pallas_call(
        functools.partial(own_kernel, patches, grid),
        out_shape=(
            jax.ShapeDtypeStruct((patches, 2 * PS, PS), F32),
            jax.ShapeDtypeStruct((patches, PS), F32),
            jax.ShapeDtypeStruct((side, side), BF16),
            jax.ShapeDtypeStruct((patches,), jnp.int32),
        ),
        in_specs=[SMEM] + [VMEM] * 4,
        out_specs=(VMEM, VMEM, ANY, SMEM),
        scratch_shapes=[
            pltpu.VMEM((patches, PS, COLS), BF16),
            pltpu.VMEM((patches, PS, PS), BF16),
            pltpu.VMEM((patches, 2 * PS, PS), BF16),
            pltpu.SemaphoreType.DMA,
        ],
        **params(20, patches * 12 * PS**3, side * side * 2),
    )(positions, picture, forward, lowest, down)

    correlations = ()
    for share, previous in zip(shares, arrivals):
        size = len(share)
        correlations = (
            pl.pallas_call(
                functools.partial(match_kernel, share),
                out_shape=jax.ShapeDtypeStruct((patches, PS, PS), F32),
                in_specs=[ANY] + [VMEM] * 7 + [ANY] * len(correlations),
                out_specs=ANY,
                scratch_shapes=[
                    pltpu.VMEM(((size + 1) // 2, 2 * PS, 2 * PS), BF16),
                    pltpu.VMEM(((size + 1) // 2, 2 * PS, 2 * PS), BF16),
                    pltpu.VMEM((size, PS, 2 * PS), BF16),
                    pltpu.VMEM((size, PS), F32),
                    pltpu.VMEM((size, PS, PS), F32),
                    pltpu.SMEM((patches,), jnp.int32),
                    pltpu.SemaphoreType.DMA((size,)),
                    pltpu.SemaphoreType.DMA,
                ],
                input_output_aliases={8: 0} if correlations else {},
                **params(16, size * 16 * PS**3, size * PS * PS * 14),
            )(order, previous, spectra, powers, forward, lowest, down, back, *correlations),
        )
    (correlations,) = correlations
    return warped[None], correlations[None]


def solution(mesh):
    return jax.shard_map(
        shards,
        mesh=mesh,
        in_specs=(
            P(("parts", "sec"), "tile", None, None),
            P(("parts", "sec"), "tile", None),
            P(("parts", "sec"), "tile", None, None),
            P(),
            P(("parts", "sec"), "tile", None),
        ),
        out_specs=(P(("parts", "sec"), "tile", None), P(("parts", "sec"), "tile", None, None)),
        check_vma=False,
    )
```

```python
import functools

import jax
import jax.numpy as jnp
import ml_dtypes
import numpy as np
from jax import lax
from jax.experimental import pallas as pl
from jax.experimental.pallas import tpu as pltpu
from jax.sharding import PartitionSpec as P

BS = 256
PS = 128
KP = 3
CAP = 12
LISTED = CAP + 1
SHIFT = 8
FIELD = 1 << SHIFT
EPSILON = 1e-06
ROWS = PS + 16
COLS = 2 * PS
LAG = 3

SMEM = pl.BlockSpec(memory_space=pltpu.SMEM)
VMEM = pl.BlockSpec(memory_space=pltpu.VMEM)
ANY = pl.BlockSpec(memory_space=pl.ANY)
F32 = jnp.float32
BF16 = jnp.bfloat16


def tables():
    grid = np.arange(PS)
    folded = np.minimum(grid, PS - grid)
    quarter = np.minimum(folded, PS // 2 - folded)
    wave = np.sign(PS // 4 - folded) * np.cos(2.0 * np.pi / PS * quarter)
    phase = grid[:, None] * grid[None, :] % PS
    cosine, sine = wave[phase], wave[(phase + 3 * PS // 4) % PS]
    across = np.concatenate([cosine, sine], axis=1)
    high = across.astype(ml_dtypes.bfloat16)
    low = (across - high.astype(np.float64)).astype(ml_dtypes.bfloat16)
    forward = np.concatenate([high, low], axis=0)
    lowest = (grid[None, :] == 0).astype(np.float32) / PS
    down = np.block([[cosine, -sine], [sine, cosine]]).astype(ml_dtypes.bfloat16)
    back = np.concatenate([cosine, -sine], axis=0).astype(ml_dtypes.bfloat16)
    return forward, lowest, down, back


def dot(a, b):
    return jnp.dot(a, b, preferred_element_type=F32)


def gate_kernel(out):
    out[...] = jnp.zeros(out.shape, out.dtype)


def early_rows(grid):
    return grid // 2 + 1


def from_top(corners, patches, grid):
    fitting = jnp.int32(0)
    for p in range(patches):
        fitting = fitting + (corners[0, p] <= early_rows(grid) * BS - PS).astype(jnp.int32)
    return fitting >= (patches + 1) // 2


def window_order(corners, order, patches, grid):
    down = jnp.where(from_top(corners, patches, grid), 0, grid - early_rows(grid))
    low = down * BS
    high = low + early_rows(grid) * BS - PS
    front, back = jnp.int32(0), jnp.int32(patches - 1)
    for p in range(patches):
        y = corners[0, p]
        early = ((y >= low) & (y <= high) & (front < (patches + 1) // 2)).astype(jnp.int32)
        order[back + early * (front - back)] = p
        front = front + early
        back = back + early - 1
    return down


def near_kernel(count, grid, ids, mats, source, table, gate, lefts, plan):
    low = lax.axis_index("tile") * count
    pulls = count * KP
    for r in range(2 * LISTED):
        plan[pulls + r] = 0
    found = jnp.int32(0)
    for block in range(count):
        for k in range(KP):
            local = ids[k, 0, block] - low
            here = (local >= 0) & (local < count)
            index = jnp.where(here, local, 0)
            slot = jnp.minimum(found, CAP)
            plan[block * KP + k] = (
                jnp.where(here, 0, slot + 1)
                + mats[k, 1, block] * FIELD
                + mats[k, 0, block] * FIELD**2
                + index * FIELD**3
            )
            plan[pulls + slot] = jnp.where(here, 0, jnp.where(local < 0, local + count, local - count))
            plan[pulls + LISTED + slot] = mats[k, 0, block]
            found = found + jnp.where(here, 0, 1)
            if grid <= block < count - grid:
                left = dot(table[mats[k, 0, block]], source[index])
                lefts[(block - grid) * KP + k] = left.astype(BF16)


def warp_row(row, inner, grid, source, table, plan, lefts, others):
    blocks = []
    for column in range(grid):
        block = row * grid + column
        total = None
        for k in range(KP):
            pull = plan[block * KP + k]
            slot, column_matrix = pull & FIELD - 1, (pull >> SHIFT) & FIELD - 1
            if inner:
                near = lefts[(block - grid) * KP + k]
            else:
                near = dot(table[(pull >> 2 * SHIFT) & FIELD - 1], source[pull >> 3 * SHIFT]).astype(BF16)
            left = jnp.where(slot == 0, near, others[jnp.maximum(slot - 1, 0)])
            term = lax.dot_general(
                left, table[column_matrix], (((1,), (1,)), ((), ())), preferred_element_type=F32
            )
            total = term if total is None else total + term
        blocks.append(total.astype(BF16))
    return blocks


def cut_windows(picture, corners, wanted, above, bands, out):
    i = lax.broadcasted_iota(jnp.int32, (PS, ROWS), 0)
    r = lax.broadcasted_iota(jnp.int32, (PS, ROWS), 1)
    c = lax.broadcasted_iota(jnp.int32, (COLS, PS), 0)
    j = lax.broadcasted_iota(jnp.int32, (COLS, PS), 1)
    rests = []
    for n, p in enumerate(wanted):
        y, x = corners[0, p] - above, corners[1, p]
        top = pl.multiple_of(jnp.minimum(y // 16 * 16, picture.shape[0] - ROWS), 16)
        left = pl.multiple_of(jnp.minimum(x // PS * PS, picture.shape[1] - COLS), PS)
        pick_rows = (r - i == y - top).astype(F32).astype(BF16)
        bands[n] = dot(pick_rows, picture[pl.ds(top, ROWS), pl.ds(left, COLS)]).astype(BF16)
        rests.append(x - left)
    for n, rest in enumerate(rests):
        pick_cols = (c - j == rest).astype(F32).astype(BF16)
        out[n] = dot(bands[n], pick_cols).astype(BF16)


def fill_row(picture, row, blocks):
    for column, block in enumerate(blocks):
        picture[pl.ds(pl.multiple_of(row * BS, BS), BS), pl.ds(column * BS, BS)] = block


def early_kernel(
    grid, patches, plan, corners, source, other, table, lefts, early, others, out, order, bands
):
    pulls = grid * grid * KP
    for r in range(CAP):
        left = dot(table[plan[pulls + LISTED + r]], other[plan[pulls + r]])
        others[r] = left.astype(BF16)
    down = window_order(corners, order, patches, grid)
    above = jnp.where(down == 0, 1, 0)
    given = source, table, plan, lefts, others
    for n in range(early_rows(grid) - 1):
        fill_row(early, n + above, warp_row(down + n + above, True, grid, *given))
    outer = jnp.where(down == 0, 0, grid - 1)
    fill_row(early, outer - down, warp_row(outer, False, grid, *given))
    cut_windows(early, corners, [order[n] for n in range(out.shape[0])], down * BS, bands, out)


def late_kernel(
    grid, patches, plan, corners, source, table, lefts, others, early, picture, out, order, bands
):
    rows = early_rows(grid)
    down = window_order(corners, order, patches, grid)
    given = source, table, plan, lefts, others
    for n in range(rows):
        picture[pl.ds(pl.multiple_of((down + n) * BS, BS), BS), :] = early[pl.ds(n * BS, BS), :]
    for n in range(grid - rows - 1):
        row = jnp.where(down == 0, rows + n, 1 + n)
        fill_row(picture, row, warp_row(row, True, grid, *given))
    outer = jnp.where(down == 0, grid - 1, 0)
    fill_row(picture, outer, warp_row(outer, False, grid, *given))
    wanted = [order[n] for n in range(patches - out.shape[0], patches)]
    cut_windows(picture, corners, wanted, 0, bands, out)


def spectrum_columns(patch, forward, lowest):
    halves = dot(jnp.concatenate([patch, patch], axis=1), forward[...])
    cosine_part, sine_part = halves[:, :PS], halves[:, PS:]
    cosine_part = cosine_part - jnp.sum(cosine_part, axis=0, keepdims=True) * lowest[...]
    return cosine_part.astype(BF16), sine_part.astype(BF16)


def energy(real, imag):
    return jnp.sum(real * real + imag * imag, axis=0, keepdims=True)


def mean_square(energies):
    return jnp.sum(energies, axis=1, keepdims=True) * (1.0 / PS**4)


def own_kernel(
    patches, grid, corners, picture, forward, lowest, down, out, power_out, warped, order, rows, bands, halves, sem
):
    write = pltpu.make_async_copy(picture, warped, sem)
    write.start()
    window_order(corners, order, patches, grid)
    cut_windows(picture, corners, [order[n] for n in range(patches)], 0, rows, bands)
    for p in range(patches):
        halves[p, :PS], halves[p, PS:] = spectrum_columns(bands[p], forward, lowest)
    for p in range(patches):
        both = dot(down[...], halves[p])
        out[p] = both
        power_out[pl.ds(p, 1), :] = energy(both[:PS], both[PS:])
    power_out[...] = jnp.broadcast_to(mean_square(power_out[...]), power_out.shape)
    write.wait()


def match_kernel(
    share, order, previous, spectra, powers, forward, lowest, down, back, *rest
):
    out, halves, crosses, mixed, scales, done, slots, sems, slots_sem = rest[-9:]
    fetch = pltpu.make_async_copy(order, slots, slots_sem)
    fetch.start()
    pairs = [share[start : start + 2] for start in range(0, len(share), 2)]
    writes = []

    def columns(q):
        for n in range(len(pairs[q])):
            at = pl.ds(n * PS, PS)
            halves[q, :PS, at], halves[q, PS:, at] = spectrum_columns(previous[2 * q + n], forward, lowest)

    def cross(q):
        pair = pairs[q]
        second = dot(down[...], halves[q, :, : PS * len(pair)])
        for n, p in enumerate(pair):
            one_real, one_imag = spectra[p, :PS, :], spectra[p, PS:, :]
            two_real, two_imag = second[:PS, n * PS : (n + 1) * PS], second[PS:, n * PS : (n + 1) * PS]
            power = mean_square(energy(two_real, two_imag))
            product = (powers[pl.ds(p, 1), :] + EPSILON) * (power + EPSILON)
            scales[pl.ds(2 * q + n, 1), :] = lax.rsqrt(product) * (1.0 / (PS * PS * PS))
            real = one_real * two_real + one_imag * two_imag
            imag = one_real * two_imag - one_imag * two_real
            crosses[q, :PS, pl.ds(n * PS, PS)] = real.astype(BF16)
            crosses[q, PS:, pl.ds(n * PS, PS)] = imag.astype(BF16)

    def mix(q):
        pair = pairs[q]
        both = dot(down[...], crosses[q, :, : PS * len(pair)]).astype(BF16)
        for n in range(len(pair)):
            mixed[2 * q + n, :, :PS] = both[:PS, n * PS : (n + 1) * PS]
            mixed[2 * q + n, :, PS:] = both[PS:, n * PS : (n + 1) * PS]

    def finish(q):
        if q == 0:
            fetch.wait()
        for n, p in enumerate(pairs[q], 2 * q):
            done[n] = dot(mixed[n], back[...]) * scales[pl.ds(n, 1), :]
            writes.append(pltpu.make_async_copy(done.at[n], out.at[slots[p]], sems.at[n]))
            writes[-1].start()

    stages = columns, cross, mix, finish
    for step in range(len(pairs) + LAG * (len(stages) - 1)):
        for s, stage in enumerate(stages):
            if 0 <= step - LAG * s < len(pairs):
                stage(step - LAG * s)
    for write in writes:
        write.wait()


def params(megabytes, flops, moved):
    return dict(
        compiler_params=pltpu.CompilerParams(vmem_limit_bytes=megabytes << 20),
        cost_estimate=pl.CostEstimate(flops=flops, bytes_accessed=moved, transcendentals=0),
    )


def shards(source, pull_ids, interp_idx, interp_table, patch_pos):
    blocks = source[0]
    count = blocks.shape[0]
    grid = int(round(count**0.5))
    patches = patch_pos.shape[1]
    side = grid * BS
    ids = pull_ids.transpose(2, 0, 1)
    mats = interp_idx[0].transpose(1, 2, 0)
    positions = patch_pos[0].T
    shares = range((patches + 1) // 2), range((patches + 1) // 2, patches)
    sections = lax.axis_size("sec")
    tiles = lax.axis_size("tile")
    other = lax.ppermute(blocks, "tile", [(i, (i + 1) % tiles) for i in range(tiles)])
    gate = pl.pallas_call(
        gate_kernel,
        out_shape=jax.ShapeDtypeStruct((8, 128), F32),
        out_specs=VMEM,
        **params(16, 2 << 30, 16 << 20),
    )()
    gate, asked = lax.optimization_barrier((gate, positions))
    wanted = lax.ppermute(asked, "sec", [(i + 1, i) for i in range(sections - 1)])
    forward, lowest, down, back = tables()

    onward = [(i, i + 1) for i in range(sections - 1)]

    pulls = count * KP
    inner = pulls - 2 * grid * KP
    lefts, plan = pl.pallas_call(
        functools.partial(near_kernel, count, grid),
        out_shape=(
            jax.ShapeDtypeStruct((inner, BS, BS), BF16),
            jax.ShapeDtypeStruct((pulls + 2 * LISTED,), jnp.int32),
        ),
        in_specs=[SMEM, SMEM, VMEM, VMEM, ANY],
        out_specs=(VMEM, SMEM),
        **params(16, inner * 2 * BS**3, (count + inner) * BS * BS * 2),
    )(ids, mats, blocks, interp_table, gate)

    rows = early_rows(grid)
    early, others, sent = pl.pallas_call(
        functools.partial(early_kernel, grid, patches),
        out_shape=(
            jax.ShapeDtypeStruct((rows * BS, side), BF16),
            jax.ShapeDtypeStruct((CAP, BS, BS), BF16),
            jax.ShapeDtypeStruct((len(shares[0]), PS, PS), BF16),
        ),
        in_specs=[SMEM] * 2 + [VMEM] * 4,
        out_specs=[VMEM] * 3,
        scratch_shapes=[pltpu.SMEM((patches,), jnp.int32), pltpu.VMEM((len(shares[0]), PS, COLS), BF16)],
        **params(16, rows * grid * KP * 2 * BS**3, rows * grid * KP * BS * BS * 4),
    )(plan, wanted, blocks, other, interp_table, lefts)
    arrivals = [lax.ppermute(sent, "sec", onward)]
    picture, sent = pl.pallas_call(
        functools.partial(late_kernel, grid, patches),
        out_shape=(
            jax.ShapeDtypeStruct((side, side), BF16),
            jax.ShapeDtypeStruct((len(shares[1]), PS, PS), BF16),
        ),
        in_specs=[SMEM] * 2 + [VMEM] * 5,
        out_specs=[VMEM] * 2,
        scratch_shapes=[pltpu.SMEM((patches,), jnp.int32), pltpu.VMEM((len(shares[0]), PS, COLS), BF16)],
        **params(16, (grid - rows) * grid * KP * 2 * BS**3, side * side * 4),
    )(plan, wanted, blocks, interp_table, lefts, others, early)
    arrivals.append(lax.ppermute(sent, "sec", onward))

    spectra, powers, warped, order = pl.pallas_call(
        functools.partial(own_kernel, patches, grid),
        out_shape=(
            jax.ShapeDtypeStruct((patches, 2 * PS, PS), F32),
            jax.ShapeDtypeStruct((patches, PS), F32),
            jax.ShapeDtypeStruct((side, side), BF16),
            jax.ShapeDtypeStruct((patches,), jnp.int32),
        ),
        in_specs=[SMEM] + [VMEM] * 4,
        out_specs=(VMEM, VMEM, ANY, SMEM),
        scratch_shapes=[
            pltpu.VMEM((patches, PS, COLS), BF16),
            pltpu.VMEM((patches, PS, PS), BF16),
            pltpu.VMEM((patches, 2 * PS, PS), BF16),
            pltpu.SemaphoreType.DMA,
        ],
        **params(20, patches * 12 * PS**3, side * side * 2),
    )(positions, picture, forward, lowest, down)

    correlations = ()
    for share, previous in zip(shares, arrivals):
        size = len(share)
        correlations = (
            pl.pallas_call(
                functools.partial(match_kernel, share),
                out_shape=jax.ShapeDtypeStruct((patches, PS, PS), F32),
                in_specs=[ANY] + [VMEM] * 7 + [ANY] * len(correlations),
                out_specs=ANY,
                scratch_shapes=[
                    pltpu.VMEM(((size + 1) // 2, 2 * PS, 2 * PS), BF16),
                    pltpu.VMEM(((size + 1) // 2, 2 * PS, 2 * PS), BF16),
                    pltpu.VMEM((size, PS, 2 * PS), BF16),
                    pltpu.VMEM((size, PS), F32),
                    pltpu.VMEM((size, PS, PS), F32),
                    pltpu.SMEM((patches,), jnp.int32),
                    pltpu.SemaphoreType.DMA((size,)),
                    pltpu.SemaphoreType.DMA,
                ],
                input_output_aliases={8: 0} if correlations else {},
                **params(16, size * 16 * PS**3, size * PS * PS * 14),
            )(order, previous, spectra, powers, forward, lowest, down, back, *correlations),
        )
    (correlations,) = correlations
    return warped[None], correlations[None]


def solution(mesh):
    return jax.shard_map(
        shards,
        mesh=mesh,
        in_specs=(
            P(("parts", "sec"), "tile", None, None),
            P(("parts", "sec"), "tile", None),
            P(("parts", "sec"), "tile", None, None),
            P(),
            P(("parts", "sec"), "tile", None),
        ),
        out_specs=(P(("parts", "sec"), "tile", None), P(("parts", "sec"), "tile", None, None)),
        check_vma=False,
    )
```

```python
import functools

import jax
import jax.numpy as jnp
import ml_dtypes
import numpy as np
from jax import lax
from jax.experimental import pallas as pl
from jax.experimental.pallas import tpu as pltpu
from jax.sharding import PartitionSpec as P

BS = 256
PS = 128
KP = 3
CAP = 12
LISTED = CAP + 1
SHIFT = 8
FIELD = 1 << SHIFT
EPSILON = 1e-06
ROWS = PS + 16
COLS = 2 * PS
LAG = 3

SMEM = pl.BlockSpec(memory_space=pltpu.SMEM)
VMEM = pl.BlockSpec(memory_space=pltpu.VMEM)
ANY = pl.BlockSpec(memory_space=pl.ANY)
F32 = jnp.float32
BF16 = jnp.bfloat16


def tables():
    grid = np.arange(PS)
    folded = np.minimum(grid, PS - grid)
    quarter = np.minimum(folded, PS // 2 - folded)
    wave = np.sign(PS // 4 - folded) * np.cos(2.0 * np.pi / PS * quarter)
    phase = grid[:, None] * grid[None, :] % PS
    cosine, sine = wave[phase], wave[(phase + 3 * PS // 4) % PS]
    across = np.concatenate([cosine, sine], axis=1)
    high = across.astype(ml_dtypes.bfloat16)
    low = (across - high.astype(np.float64)).astype(ml_dtypes.bfloat16)
    forward = np.concatenate([high, low], axis=0)
    lowest = (grid[None, :] == 0).astype(np.float32) / PS
    down = np.block([[cosine, -sine], [sine, cosine]]).astype(ml_dtypes.bfloat16)
    back = np.concatenate([cosine, -sine], axis=0).astype(ml_dtypes.bfloat16)
    return forward, lowest, down, back


def dot(a, b):
    return jnp.dot(a, b, preferred_element_type=F32)


def gate_kernel(out):
    out[...] = jnp.zeros(out.shape, out.dtype)


def early_rows(grid):
    return grid // 2 + 1


def always_early(row, grid):
    return grid - early_rows(grid) <= row < early_rows(grid)


def from_top(corners, patches, grid):
    fitting = jnp.int32(0)
    for p in range(patches):
        fitting = fitting + (corners[0, p] <= early_rows(grid) * BS - PS).astype(jnp.int32)
    return fitting >= (patches + 1) // 2


def window_order(corners, order, patches, grid):
    down = jnp.where(from_top(corners, patches, grid), 0, grid - early_rows(grid))
    low = down * BS
    high = low + early_rows(grid) * BS - PS
    front, back = jnp.int32(0), jnp.int32(patches - 1)
    for p in range(patches):
        y = corners[0, p]
        early = ((y >= low) & (y <= high) & (front < (patches + 1) // 2)).astype(jnp.int32)
        order[back + early * (front - back)] = p
        front = front + early
        back = back + early - 1
    return down


def near_kernel(count, grid, ids, mats, source, table, gate, lefts, plan):
    low = lax.axis_index("tile") * count
    pulls = count * KP
    for r in range(2 * LISTED):
        plan[pulls + r] = 0
    found = jnp.int32(0)
    for block in range(count):
        for k in range(KP):
            local = ids[k, 0, block] - low
            here = (local >= 0) & (local < count)
            index = jnp.where(here, local, 0)
            slot = jnp.minimum(found, CAP)
            plan[block * KP + k] = (
                jnp.where(here, 0, slot + 1)
                + mats[k, 1, block] * FIELD
                + mats[k, 0, block] * FIELD**2
                + index * FIELD**3
            )
            plan[pulls + slot] = jnp.where(here, 0, jnp.where(local < 0, local + count, local - count))
            plan[pulls + LISTED + slot] = mats[k, 0, block]
            found = found + jnp.where(here, 0, 1)
            if always_early(block // grid, grid):
                left = dot(table[mats[k, 0, block]], source[index])
                lefts[(block - (grid - early_rows(grid)) * grid) * KP + k] = left.astype(BF16)


def warp_row(row, inner, grid, source, table, plan, lefts, others):
    blocks = []
    for column in range(grid):
        block = row * grid + column
        total = None
        for k in range(KP):
            pull = plan[block * KP + k]
            slot, column_matrix = pull & FIELD - 1, (pull >> SHIFT) & FIELD - 1
            if inner:
                near = lefts[(block - (grid - early_rows(grid)) * grid) * KP + k]
            else:
                near = dot(table[(pull >> 2 * SHIFT) & FIELD - 1], source[pull >> 3 * SHIFT]).astype(BF16)
            left = jnp.where(slot == 0, near, others[jnp.maximum(slot - 1, 0)])
            term = lax.dot_general(
                left, table[column_matrix], (((1,), (1,)), ((), ())), preferred_element_type=F32
            )
            total = term if total is None else total + term
        blocks.append(total.astype(BF16))
    return blocks


def cut_windows(picture, corners, wanted, above, bands, out):
    i = lax.broadcasted_iota(jnp.int32, (PS, ROWS), 0)
    r = lax.broadcasted_iota(jnp.int32, (PS, ROWS), 1)
    c = lax.broadcasted_iota(jnp.int32, (COLS, PS), 0)
    j = lax.broadcasted_iota(jnp.int32, (COLS, PS), 1)
    rests = []
    for n, p in enumerate(wanted):
        y, x = corners[0, p] - above, corners[1, p]
        top = pl.multiple_of(jnp.minimum(y // 16 * 16, picture.shape[0] - ROWS), 16)
        left = pl.multiple_of(jnp.minimum(x // PS * PS, picture.shape[1] - COLS), PS)
        pick_rows = (r - i == y - top).astype(F32).astype(BF16)
        bands[n] = dot(pick_rows, picture[pl.ds(top, ROWS), pl.ds(left, COLS)]).astype(BF16)
        rests.append(x - left)
    for n, rest in enumerate(rests):
        pick_cols = (c - j == rest).astype(F32).astype(BF16)
        out[n] = dot(bands[n], pick_cols).astype(BF16)


def fill_row(picture, row, blocks):
    for column, block in enumerate(blocks):
        picture[pl.ds(pl.multiple_of(row * BS, BS), BS), pl.ds(column * BS, BS)] = block


def early_kernel(
    grid, patches, plan, corners, source, other, table, lefts, early, others, out, order, bands
):
    pulls = grid * grid * KP
    for r in range(CAP):
        left = dot(table[plan[pulls + LISTED + r]], other[plan[pulls + r]])
        others[r] = left.astype(BF16)
    down = window_order(corners, order, patches, grid)
    given = source, table, plan, lefts, others
    for row in range(grid):
        if always_early(row, grid):
            fill_row(early, row - down, warp_row(row, True, grid, *given))
    outer = jnp.where(down == 0, 0, early_rows(grid))
    for n in range(grid - early_rows(grid)):
        fill_row(early, outer + n - down, warp_row(outer + n, False, grid, *given))
    cut_windows(early, corners, [order[n] for n in range(out.shape[0])], down * BS, bands, out)


def late_kernel(
    grid, patches, plan, corners, source, table, lefts, others, early, picture, out, order, bands
):
    rows = early_rows(grid)
    down = window_order(corners, order, patches, grid)
    given = source, table, plan, lefts, others
    for n in range(rows):
        picture[pl.ds(pl.multiple_of((down + n) * BS, BS), BS), :] = early[pl.ds(n * BS, BS), :]
    outer = jnp.where(down == 0, rows, 0)
    for n in range(grid - rows):
        fill_row(picture, outer + n, warp_row(outer + n, False, grid, *given))
    wanted = [order[n] for n in range(patches - out.shape[0], patches)]
    cut_windows(picture, corners, wanted, 0, bands, out)


def spectrum_columns(patch, forward, lowest):
    halves = dot(jnp.concatenate([patch, patch], axis=1), forward[...])
    cosine_part, sine_part = halves[:, :PS], halves[:, PS:]
    cosine_part = cosine_part - jnp.sum(cosine_part, axis=0, keepdims=True) * lowest[...]
    return cosine_part.astype(BF16), sine_part.astype(BF16)


def energy(real, imag):
    return jnp.sum(real * real + imag * imag, axis=0, keepdims=True)


def mean_square(energies):
    return jnp.sum(energies, axis=1, keepdims=True) * (1.0 / PS**4)


def own_kernel(
    patches, grid, corners, picture, forward, lowest, down, out, power_out, warped, order, rows, bands, halves, sem
):
    write = pltpu.make_async_copy(picture, warped, sem)
    write.start()
    window_order(corners, order, patches, grid)
    cut_windows(picture, corners, [order[n] for n in range(patches)], 0, rows, bands)
    for p in range(patches):
        halves[p, :PS], halves[p, PS:] = spectrum_columns(bands[p], forward, lowest)
    for p in range(patches):
        both = dot(down[...], halves[p])
        out[p] = both
        power_out[pl.ds(p, 1), :] = energy(both[:PS], both[PS:])
    power_out[...] = jnp.broadcast_to(mean_square(power_out[...]), power_out.shape)
    write.wait()


def match_kernel(
    share, order, previous, spectra, powers, forward, lowest, down, back, *rest
):
    out, halves, crosses, mixed, scales, done, slots, sems, slots_sem = rest[-9:]
    fetch = pltpu.make_async_copy(order, slots, slots_sem)
    fetch.start()
    pairs = [share[start : start + 2] for start in range(0, len(share), 2)]
    writes = []

    def columns(q):
        for n in range(len(pairs[q])):
            at = pl.ds(n * PS, PS)
            halves[q, :PS, at], halves[q, PS:, at] = spectrum_columns(previous[2 * q + n], forward, lowest)

    def cross(q):
        pair = pairs[q]
        second = dot(down[...], halves[q, :, : PS * len(pair)])
        for n, p in enumerate(pair):
            one_real, one_imag = spectra[p, :PS, :], spectra[p, PS:, :]
            two_real, two_imag = second[:PS, n * PS : (n + 1) * PS], second[PS:, n * PS : (n + 1) * PS]
            power = mean_square(energy(two_real, two_imag))
            product = (powers[pl.ds(p, 1), :] + EPSILON) * (power + EPSILON)
            scales[pl.ds(2 * q + n, 1), :] = lax.rsqrt(product) * (1.0 / (PS * PS * PS))
            real = one_real * two_real + one_imag * two_imag
            imag = one_real * two_imag - one_imag * two_real
            crosses[q, :PS, pl.ds(n * PS, PS)] = real.astype(BF16)
            crosses[q, PS:, pl.ds(n * PS, PS)] = imag.astype(BF16)

    def mix(q):
        pair = pairs[q]
        both = dot(down[...], crosses[q, :, : PS * len(pair)]).astype(BF16)
        for n in range(len(pair)):
            mixed[2 * q + n, :, :PS] = both[:PS, n * PS : (n + 1) * PS]
            mixed[2 * q + n, :, PS:] = both[PS:, n * PS : (n + 1) * PS]

    def finish(q):
        if q == 0:
            fetch.wait()
        for n, p in enumerate(pairs[q], 2 * q):
            done[n] = dot(mixed[n], back[...]) * scales[pl.ds(n, 1), :]
            writes.append(pltpu.make_async_copy(done.at[n], out.at[slots[p]], sems.at[n]))
            writes[-1].start()

    stages = columns, cross, mix, finish
    for step in range(len(pairs) + LAG * (len(stages) - 1)):
        for s, stage in enumerate(stages):
            if 0 <= step - LAG * s < len(pairs):
                stage(step - LAG * s)
    for write in writes:
        write.wait()


def params(megabytes, flops, moved):
    return dict(
        compiler_params=pltpu.CompilerParams(vmem_limit_bytes=megabytes << 20),
        cost_estimate=pl.CostEstimate(flops=flops, bytes_accessed=moved, transcendentals=0),
    )


def shards(source, pull_ids, interp_idx, interp_table, patch_pos):
    blocks = source[0]
    count = blocks.shape[0]
    grid = int(round(count**0.5))
    patches = patch_pos.shape[1]
    side = grid * BS
    ids = pull_ids.transpose(2, 0, 1)
    mats = interp_idx[0].transpose(1, 2, 0)
    positions = patch_pos[0].T
    shares = range((patches + 1) // 2), range((patches + 1) // 2, patches)
    sections = lax.axis_size("sec")
    tiles = lax.axis_size("tile")
    other = lax.ppermute(blocks, "tile", [(i, (i + 1) % tiles) for i in range(tiles)])
    gate = pl.pallas_call(
        gate_kernel,
        out_shape=jax.ShapeDtypeStruct((8, 128), F32),
        out_specs=VMEM,
        **params(16, 2 << 30, 16 << 20),
    )()
    gate, asked = lax.optimization_barrier((gate, positions))
    wanted = lax.ppermute(asked, "sec", [(i + 1, i) for i in range(sections - 1)])
    forward, lowest, down, back = tables()

    onward = [(i, i + 1) for i in range(sections - 1)]

    pulls = count * KP
    inner = (2 * early_rows(grid) - grid) * grid * KP
    lefts, plan = pl.pallas_call(
        functools.partial(near_kernel, count, grid),
        out_shape=(
            jax.ShapeDtypeStruct((inner, BS, BS), BF16),
            jax.ShapeDtypeStruct((pulls + 2 * LISTED,), jnp.int32),
        ),
        in_specs=[SMEM, SMEM, VMEM, VMEM, ANY],
        out_specs=(VMEM, SMEM),
        **params(16, inner * 2 * BS**3, (count + inner) * BS * BS * 2),
    )(ids, mats, blocks, interp_table, gate)

    rows = early_rows(grid)
    early, others, sent = pl.pallas_call(
        functools.partial(early_kernel, grid, patches),
        out_shape=(
            jax.ShapeDtypeStruct((rows * BS, side), BF16),
            jax.ShapeDtypeStruct((CAP, BS, BS), BF16),
            jax.ShapeDtypeStruct((len(shares[0]), PS, PS), BF16),
        ),
        in_specs=[SMEM] * 2 + [VMEM] * 4,
        out_specs=[VMEM] * 3,
        scratch_shapes=[pltpu.SMEM((patches,), jnp.int32), pltpu.VMEM((len(shares[0]), PS, COLS), BF16)],
        **params(16, rows * grid * KP * 2 * BS**3, rows * grid * KP * BS * BS * 4),
    )(plan, wanted, blocks, other, interp_table, lefts)
    arrivals = [lax.ppermute(sent, "sec", onward)]
    picture, sent = pl.pallas_call(
        functools.partial(late_kernel, grid, patches),
        out_shape=(
            jax.ShapeDtypeStruct((side, side), BF16),
            jax.ShapeDtypeStruct((len(shares[1]), PS, PS), BF16),
        ),
        in_specs=[SMEM] * 2 + [VMEM] * 5,
        out_specs=[VMEM] * 2,
        scratch_shapes=[pltpu.SMEM((patches,), jnp.int32), pltpu.VMEM((len(shares[0]), PS, COLS), BF16)],
        **params(16, (grid - rows) * grid * KP * 2 * BS**3, side * side * 4),
    )(plan, wanted, blocks, interp_table, lefts, others, early)
    arrivals.append(lax.ppermute(sent, "sec", onward))

    spectra, powers, warped, order = pl.pallas_call(
        functools.partial(own_kernel, patches, grid),
        out_shape=(
            jax.ShapeDtypeStruct((patches, 2 * PS, PS), F32),
            jax.ShapeDtypeStruct((patches, PS), F32),
            jax.ShapeDtypeStruct((side, side), BF16),
            jax.ShapeDtypeStruct((patches,), jnp.int32),
        ),
        in_specs=[SMEM] + [VMEM] * 4,
        out_specs=(VMEM, VMEM, ANY, SMEM),
        scratch_shapes=[
            pltpu.VMEM((patches, PS, COLS), BF16),
            pltpu.VMEM((patches, PS, PS), BF16),
            pltpu.VMEM((patches, 2 * PS, PS), BF16),
            pltpu.SemaphoreType.DMA,
        ],
        **params(20, patches * 12 * PS**3, side * side * 2),
    )(positions, picture, forward, lowest, down)

    correlations = ()
    for share, previous in zip(shares, arrivals):
        size = len(share)
        correlations = (
            pl.pallas_call(
                functools.partial(match_kernel, share),
                out_shape=jax.ShapeDtypeStruct((patches, PS, PS), F32),
                in_specs=[ANY] + [VMEM] * 7 + [ANY] * len(correlations),
                out_specs=ANY,
                scratch_shapes=[
                    pltpu.VMEM(((size + 1) // 2, 2 * PS, 2 * PS), BF16),
                    pltpu.VMEM(((size + 1) // 2, 2 * PS, 2 * PS), BF16),
                    pltpu.VMEM((size, PS, 2 * PS), BF16),
                    pltpu.VMEM((size, PS), F32),
                    pltpu.VMEM((size, PS, PS), F32),
                    pltpu.SMEM((patches,), jnp.int32),
                    pltpu.SemaphoreType.DMA((size,)),
                    pltpu.SemaphoreType.DMA,
                ],
                input_output_aliases={8: 0} if correlations else {},
                **params(16, size * 16 * PS**3, size * PS * PS * 14),
            )(order, previous, spectra, powers, forward, lowest, down, back, *correlations),
        )
    (correlations,) = correlations
    return warped[None], correlations[None]


def solution(mesh):
    return jax.shard_map(
        shards,
        mesh=mesh,
        in_specs=(
            P(("parts", "sec"), "tile", None, None),
            P(("parts", "sec"), "tile", None),
            P(("parts", "sec"), "tile", None, None),
            P(),
            P(("parts", "sec"), "tile", None),
        ),
        out_specs=(P(("parts", "sec"), "tile", None), P(("parts", "sec"), "tile", None, None)),
        check_vma=False,
    )
```

```python
import functools

import jax
import jax.numpy as jnp
import ml_dtypes
import numpy as np
from jax import lax
from jax.experimental import pallas as pl
from jax.experimental.pallas import tpu as pltpu
from jax.sharding import PartitionSpec as P

BS = 256
PS = 128
KP = 3
CAP = 12
LISTED = CAP + 1
SHIFT = 8
FIELD = 1 << SHIFT
EPSILON = 1e-06
ROWS = PS + 16
COLS = 2 * PS
LAG = 3

SMEM = pl.BlockSpec(memory_space=pltpu.SMEM)
VMEM = pl.BlockSpec(memory_space=pltpu.VMEM)
ANY = pl.BlockSpec(memory_space=pl.ANY)
F32 = jnp.float32
BF16 = jnp.bfloat16


def tables():
    grid = np.arange(PS)
    folded = np.minimum(grid, PS - grid)
    quarter = np.minimum(folded, PS // 2 - folded)
    wave = np.sign(PS // 4 - folded) * np.cos(2.0 * np.pi / PS * quarter)
    phase = grid[:, None] * grid[None, :] % PS
    cosine, sine = wave[phase], wave[(phase + 3 * PS // 4) % PS]
    across = np.concatenate([cosine, sine], axis=1)
    high = across.astype(ml_dtypes.bfloat16)
    low = (across - high.astype(np.float64)).astype(ml_dtypes.bfloat16)
    forward = np.concatenate([high, low], axis=0)
    lowest = (grid[None, :] == 0).astype(np.float32) / PS
    down = np.block([[cosine, -sine], [sine, cosine]]).astype(ml_dtypes.bfloat16)
    back = np.concatenate([cosine, -sine], axis=0).astype(ml_dtypes.bfloat16)
    return forward, lowest, down, back


def dot(a, b):
    return jnp.dot(a, b, preferred_element_type=F32)


def gate_kernel(out):
    out[...] = jnp.zeros(out.shape, out.dtype)


def early_rows(grid):
    return grid // 2 + 1


def always_early(row, grid):
    return grid - early_rows(grid) <= row < early_rows(grid)


def from_top(corners, patches, grid):
    fitting = jnp.int32(0)
    for p in range(patches):
        fitting = fitting + (corners[0, p] <= early_rows(grid) * BS - PS).astype(jnp.int32)
    return fitting >= (patches + 1) // 2


def window_order(corners, order, patches, grid):
    down = jnp.where(from_top(corners, patches, grid), 0, grid - early_rows(grid))
    low = down * BS
    high = low + early_rows(grid) * BS - PS
    front, back = jnp.int32(0), jnp.int32(patches - 1)
    for p in range(patches):
        y = corners[0, p]
        early = ((y >= low) & (y <= high) & (front < (patches + 1) // 2)).astype(jnp.int32)
        order[back + early * (front - back)] = p
        front = front + early
        back = back + early - 1
    return down


def near_kernel(count, grid, ids, mats, source, table, gate, lefts, plan):
    low = lax.axis_index("tile") * count
    pulls = count * KP
    for r in range(2 * LISTED):
        plan[pulls + r] = 0
    found = jnp.int32(0)
    for block in range(count):
        for k in range(KP):
            local = ids[k, 0, block] - low
            here = (local >= 0) & (local < count)
            index = jnp.where(here, local, 0)
            slot = jnp.minimum(found, CAP)
            plan[block * KP + k] = (
                jnp.where(here, 0, slot + 1)
                + mats[k, 1, block] * FIELD
                + mats[k, 0, block] * FIELD**2
                + index * FIELD**3
            )
            plan[pulls + slot] = jnp.where(here, 0, jnp.where(local < 0, local + count, local - count))
            plan[pulls + LISTED + slot] = mats[k, 0, block]
            found = found + jnp.where(here, 0, 1)
            if always_early(block // grid, grid):
                left = dot(table[mats[k, 0, block]], source[index])
                lefts[(block - (grid - early_rows(grid)) * grid) * KP + k] = left.astype(BF16)


def warp_row(row, inner, grid, source, table, plan, lefts, others):
    blocks = []
    for column in range(grid):
        block = row * grid + column
        total = None
        for k in range(KP):
            pull = plan[block * KP + k]
            slot, column_matrix = pull & FIELD - 1, (pull >> SHIFT) & FIELD - 1
            if inner:
                near = lefts[(block - (grid - early_rows(grid)) * grid) * KP + k]
            else:
                near = dot(table[(pull >> 2 * SHIFT) & FIELD - 1], source[pull >> 3 * SHIFT]).astype(BF16)
            left = jnp.where(slot == 0, near, others[jnp.maximum(slot - 1, 0)])
            term = lax.dot_general(
                left, table[column_matrix], (((1,), (1,)), ((), ())), preferred_element_type=F32
            )
            total = term if total is None else total + term
        blocks.append(total.astype(BF16))
    return blocks


def cut_windows(picture, corners, wanted, above, bands, out):
    i = lax.broadcasted_iota(jnp.int32, (PS, ROWS), 0)
    r = lax.broadcasted_iota(jnp.int32, (PS, ROWS), 1)
    c = lax.broadcasted_iota(jnp.int32, (COLS, PS), 0)
    j = lax.broadcasted_iota(jnp.int32, (COLS, PS), 1)
    rests = []
    for n, p in enumerate(wanted):
        y, x = corners[0, p] - above, corners[1, p]
        top = pl.multiple_of(jnp.minimum(y // 16 * 16, picture.shape[0] - ROWS), 16)
        left = pl.multiple_of(jnp.minimum(x // PS * PS, picture.shape[1] - COLS), PS)
        pick_rows = (r - i == y - top).astype(F32).astype(BF16)
        bands[n] = dot(pick_rows, picture[pl.ds(top, ROWS), pl.ds(left, COLS)]).astype(BF16)
        rests.append(x - left)
    for n, rest in enumerate(rests):
        pick_cols = (c - j == rest).astype(F32).astype(BF16)
        out[n] = dot(bands[n], pick_cols).astype(BF16)


def fill_row(picture, row, blocks):
    for column, block in enumerate(blocks):
        picture[pl.ds(pl.multiple_of(row * BS, BS), BS), pl.ds(column * BS, BS)] = block


def early_kernel(
    grid, patches, plan, corners, source, other, table, lefts, early, others, out, order, bands
):
    pulls = grid * grid * KP
    for r in range(CAP):
        left = dot(table[plan[pulls + LISTED + r]], other[plan[pulls + r]])
        others[r] = left.astype(BF16)
    down = window_order(corners, order, patches, grid)
    given = source, table, plan, lefts, others
    outer = jnp.where(down == 0, 0, early_rows(grid))
    for n in range(grid - early_rows(grid)):
        fill_row(early, outer + n - down, warp_row(outer + n, False, grid, *given))
    for row in range(grid):
        if always_early(row, grid):
            fill_row(early, row - down, warp_row(row, True, grid, *given))
    cut_windows(early, corners, [order[n] for n in range(out.shape[0])], down * BS, bands, out)


def late_kernel(
    grid, patches, plan, corners, source, table, lefts, others, early, picture, out, order, bands
):
    rows = early_rows(grid)
    down = window_order(corners, order, patches, grid)
    given = source, table, plan, lefts, others
    for n in range(rows):
        picture[pl.ds(pl.multiple_of((down + n) * BS, BS), BS), :] = early[pl.ds(n * BS, BS), :]
    outer = jnp.where(down == 0, rows, 0)
    for n in range(grid - rows):
        fill_row(picture, outer + n, warp_row(outer + n, False, grid, *given))
    wanted = [order[n] for n in range(patches - out.shape[0], patches)]
    cut_windows(picture, corners, wanted, 0, bands, out)


def spectrum_columns(patch, forward, lowest):
    halves = dot(jnp.concatenate([patch, patch], axis=1), forward[...])
    cosine_part, sine_part = halves[:, :PS], halves[:, PS:]
    cosine_part = cosine_part - jnp.sum(cosine_part, axis=0, keepdims=True) * lowest[...]
    return cosine_part.astype(BF16), sine_part.astype(BF16)


def energy(real, imag):
    return jnp.sum(real * real + imag * imag, axis=0, keepdims=True)


def mean_square(energies):
    return jnp.sum(energies, axis=1, keepdims=True) * (1.0 / PS**4)


def own_kernel(
    patches, grid, corners, picture, forward, lowest, down, out, power_out, warped, order, rows, bands, halves, sem
):
    write = pltpu.make_async_copy(picture, warped, sem)
    write.start()
    window_order(corners, order, patches, grid)
    cut_windows(picture, corners, [order[n] for n in range(patches)], 0, rows, bands)
    for p in range(patches):
        halves[p, :PS], halves[p, PS:] = spectrum_columns(bands[p], forward, lowest)
    for p in range(patches):
        both = dot(down[...], halves[p])
        out[p] = both
        power_out[pl.ds(p, 1), :] = energy(both[:PS], both[PS:])
    power_out[...] = jnp.broadcast_to(mean_square(power_out[...]), power_out.shape)
    write.wait()


def match_kernel(
    share, order, previous, spectra, powers, forward, lowest, down, back, *rest
):
    out, halves, crosses, mixed, scales, done, slots, sems, slots_sem = rest[-9:]
    fetch = pltpu.make_async_copy(order, slots, slots_sem)
    fetch.start()
    pairs = [share[start : start + 2] for start in range(0, len(share), 2)]
    writes = []

    def columns(q):
        for n in range(len(pairs[q])):
            at = pl.ds(n * PS, PS)
            halves[q, :PS, at], halves[q, PS:, at] = spectrum_columns(previous[2 * q + n], forward, lowest)

    def cross(q):
        pair = pairs[q]
        second = dot(down[...], halves[q, :, : PS * len(pair)])
        for n, p in enumerate(pair):
            one_real, one_imag = spectra[p, :PS, :], spectra[p, PS:, :]
            two_real, two_imag = second[:PS, n * PS : (n + 1) * PS], second[PS:, n * PS : (n + 1) * PS]
            power = mean_square(energy(two_real, two_imag))
            product = (powers[pl.ds(p, 1), :] + EPSILON) * (power + EPSILON)
            scales[pl.ds(2 * q + n, 1), :] = lax.rsqrt(product) * (1.0 / (PS * PS * PS))
            real = one_real * two_real + one_imag * two_imag
            imag = one_real * two_imag - one_imag * two_real
            crosses[q, :PS, pl.ds(n * PS, PS)] = real.astype(BF16)
            crosses[q, PS:, pl.ds(n * PS, PS)] = imag.astype(BF16)

    def mix(q):
        pair = pairs[q]
        both = dot(down[...], crosses[q, :, : PS * len(pair)]).astype(BF16)
        for n in range(len(pair)):
            mixed[2 * q + n, :, :PS] = both[:PS, n * PS : (n + 1) * PS]
            mixed[2 * q + n, :, PS:] = both[PS:, n * PS : (n + 1) * PS]

    def finish(q):
        if q == 0:
            fetch.wait()
        for n, p in enumerate(pairs[q], 2 * q):
            done[n] = dot(mixed[n], back[...]) * scales[pl.ds(n, 1), :]
            writes.append(pltpu.make_async_copy(done.at[n], out.at[slots[p]], sems.at[n]))
            writes[-1].start()

    stages = columns, cross, mix, finish
    for step in range(len(pairs) + LAG * (len(stages) - 1)):
        for s, stage in enumerate(stages):
            if 0 <= step - LAG * s < len(pairs):
                stage(step - LAG * s)
    for write in writes:
        write.wait()


def params(megabytes, flops, moved):
    return dict(
        compiler_params=pltpu.CompilerParams(vmem_limit_bytes=megabytes << 20),
        cost_estimate=pl.CostEstimate(flops=flops, bytes_accessed=moved, transcendentals=0),
    )


def shards(source, pull_ids, interp_idx, interp_table, patch_pos):
    blocks = source[0]
    count = blocks.shape[0]
    grid = int(round(count**0.5))
    patches = patch_pos.shape[1]
    side = grid * BS
    ids = pull_ids.transpose(2, 0, 1)
    mats = interp_idx[0].transpose(1, 2, 0)
    positions = patch_pos[0].T
    shares = range((patches + 1) // 2), range((patches + 1) // 2, patches)
    sections = lax.axis_size("sec")
    tiles = lax.axis_size("tile")
    other = lax.ppermute(blocks, "tile", [(i, (i + 1) % tiles) for i in range(tiles)])
    gate = pl.pallas_call(
        gate_kernel,
        out_shape=jax.ShapeDtypeStruct((8, 128), F32),
        out_specs=VMEM,
        **params(16, 2 << 30, 16 << 20),
    )()
    gate, asked = lax.optimization_barrier((gate, positions))
    wanted = lax.ppermute(asked, "sec", [(i + 1, i) for i in range(sections - 1)])
    forward, lowest, down, back = tables()

    onward = [(i, i + 1) for i in range(sections - 1)]

    pulls = count * KP
    inner = (2 * early_rows(grid) - grid) * grid * KP
    lefts, plan = pl.pallas_call(
        functools.partial(near_kernel, count, grid),
        out_shape=(
            jax.ShapeDtypeStruct((inner, BS, BS), BF16),
            jax.ShapeDtypeStruct((pulls + 2 * LISTED,), jnp.int32),
        ),
        in_specs=[SMEM, SMEM, VMEM, VMEM, ANY],
        out_specs=(VMEM, SMEM),
        **params(16, inner * 2 * BS**3, (count + inner) * BS * BS * 2),
    )(ids, mats, blocks, interp_table, gate)

    rows = early_rows(grid)
    early, others, sent = pl.pallas_call(
        functools.partial(early_kernel, grid, patches),
        out_shape=(
            jax.ShapeDtypeStruct((rows * BS, side), BF16),
            jax.ShapeDtypeStruct((CAP, BS, BS), BF16),
            jax.ShapeDtypeStruct((len(shares[0]), PS, PS), BF16),
        ),
        in_specs=[SMEM] * 2 + [VMEM] * 4,
        out_specs=[VMEM] * 3,
        scratch_shapes=[pltpu.SMEM((patches,), jnp.int32), pltpu.VMEM((len(shares[0]), PS, COLS), BF16)],
        **params(16, rows * grid * KP * 2 * BS**3, rows * grid * KP * BS * BS * 4),
    )(plan, wanted, blocks, other, interp_table, lefts)
    arrivals = [lax.ppermute(sent, "sec", onward)]
    picture, sent = pl.pallas_call(
        functools.partial(late_kernel, grid, patches),
        out_shape=(
            jax.ShapeDtypeStruct((side, side), BF16),
            jax.ShapeDtypeStruct((len(shares[1]), PS, PS), BF16),
        ),
        in_specs=[SMEM] * 2 + [VMEM] * 5,
        out_specs=[VMEM] * 2,
        scratch_shapes=[pltpu.SMEM((patches,), jnp.int32), pltpu.VMEM((len(shares[0]), PS, COLS), BF16)],
        **params(16, (grid - rows) * grid * KP * 2 * BS**3, side * side * 4),
    )(plan, wanted, blocks, interp_table, lefts, others, early)
    arrivals.append(lax.ppermute(sent, "sec", onward))

    spectra, powers, warped, order = pl.pallas_call(
        functools.partial(own_kernel, patches, grid),
        out_shape=(
            jax.ShapeDtypeStruct((patches, 2 * PS, PS), F32),
            jax.ShapeDtypeStruct((patches, PS), F32),
            jax.ShapeDtypeStruct((side, side), BF16),
            jax.ShapeDtypeStruct((patches,), jnp.int32),
        ),
        in_specs=[SMEM] + [VMEM] * 4,
        out_specs=(VMEM, VMEM, ANY, SMEM),
        scratch_shapes=[
            pltpu.VMEM((patches, PS, COLS), BF16),
            pltpu.VMEM((patches, PS, PS), BF16),
            pltpu.VMEM((patches, 2 * PS, PS), BF16),
            pltpu.SemaphoreType.DMA,
        ],
        **params(20, patches * 12 * PS**3, side * side * 2),
    )(positions, picture, forward, lowest, down)

    correlations = ()
    for share, previous in zip(shares, arrivals):
        size = len(share)
        correlations = (
            pl.pallas_call(
                functools.partial(match_kernel, share),
                out_shape=jax.ShapeDtypeStruct((patches, PS, PS), F32),
                in_specs=[ANY] + [VMEM] * 7 + [ANY] * len(correlations),
                out_specs=ANY,
                scratch_shapes=[
                    pltpu.VMEM(((size + 1) // 2, 2 * PS, 2 * PS), BF16),
                    pltpu.VMEM(((size + 1) // 2, 2 * PS, 2 * PS), BF16),
                    pltpu.VMEM((size, PS, 2 * PS), BF16),
                    pltpu.VMEM((size, PS), F32),
                    pltpu.VMEM((size, PS, PS), F32),
                    pltpu.SMEM((patches,), jnp.int32),
                    pltpu.SemaphoreType.DMA((size,)),
                    pltpu.SemaphoreType.DMA,
                ],
                input_output_aliases={8: 0} if correlations else {},
                **params(16, size * 16 * PS**3, size * PS * PS * 14),
            )(order, previous, spectra, powers, forward, lowest, down, back, *correlations),
        )
    (correlations,) = correlations
    return warped[None], correlations[None]


def solution(mesh):
    return jax.shard_map(
        shards,
        mesh=mesh,
        in_specs=(
            P(("parts", "sec"), "tile", None, None),
            P(("parts", "sec"), "tile", None),
            P(("parts", "sec"), "tile", None, None),
            P(),
            P(("parts", "sec"), "tile", None),
        ),
        out_specs=(P(("parts", "sec"), "tile", None), P(("parts", "sec"), "tile", None, None)),
        check_vma=False,
    )
```
